32 devices in a mesh: grp: 2 (over y), row: 4 (over z), col: 4 (over x, core).
Axes of the slice: x: 2, y: 2, z: 4, core: 2. Of those that a mesh axis runs over, the one named last changes fastest.
Arguments:
- pair: float32 [80, 40, 128], P(('grp', 'row'), 'col'), parts along dimension 0, may hold values from -6 to 6
- pair_mask: int32 [80, 40], P(('grp', 'row'), 'col'), parts along dimension 0, may hold values 0 or 1
- out_proj: float32 [128, 512], replicated, may hold values from -0.5 to 0.5
- out_gate: float32 [128, 128], replicated, may hold values from -0.5 to 0.5
- out_final: float32 [128, 128], replicated, may hold values from -0.5 to 0.5
- in_proj: float32 [128, 512], replicated, may hold values from -0.5 to 0.5
- in_gate: float32 [128, 128], replicated, may hold values from -0.5 to 0.5
- in_final: float32 [128, 128], replicated, may hold values from -0.5 to 0.5
Outputs:
- new_pair: float32 [80, 40, 128], P(('grp', 'row'), 'col'), parts along dimension 0
The draws below stay inside these ranges and needn't reach their ends.
There are 2 independent parts, one for each index of `grp`. The reference program is written for one: setup_inputs(seed, part) draws one part's arguments, and reference() takes and returns one part's arrays. A program takes and returns all parts, laid end to end along the dimension named above; an argument that names none is the same for every part. Nothing has to cross between parts.
All inputs are finite; a program needn't handle non-finite values. No bound on the sum of `pair_mask` on one device may be relied on, other than what follows from the above.
Results may differ from the reference program's by a relative error of at most 0.0075.
Values may be sent and summed in bfloat16 or wider, within the bound.
No kernel may reach another device: no remote copies, remote signals or barrier semaphores. Data moves between devices by JAX's collectives and lax.ppermute only.
A program may use at most 64 MiB of HBM per device.

```python
import jax
import jax.numpy as jnp
from jax import lax

C = 128
H = 128
TOKENS = 40
N_ROW = 4
N_COL = 4


def with_ends(values, stream_key, least, high):
    place = [jax.random.randint(jax.random.fold_in(stream_key, axis), (), 0, length) for axis, length in enumerate(values.shape)]
    widest = values.shape.index(max(values.shape))
    neighbour = place[:widest] + [(place[widest] + 1) % values.shape[widest]] + place[widest + 1:]
    return values.at[tuple(place)].set(least).at[tuple(neighbour)].set(high)


def steps_of(stream_key, extent, split, low, largest):
    gain, own = 1.0, jax.random.fold_in(stream_key, 6)
    for position, parts in split:
        heights = jnp.exp(jax.random.uniform(jax.random.fold_in(own, position), (parts,), jnp.float32, low / len(split), largest / len(split)))
        gain = gain * jnp.repeat(heights, extent[position] // parts).reshape([-1 if axis == position else 1 for axis in range(len(extent))])
    return gain


def bell_draw(rng, shape, deviation, bound, shards=(), held_as=jnp.bfloat16):
    entries = jax.random.normal(rng, shape, jnp.float32) * deviation
    if len(shards) > 0:
        entries = steps_of(rng, shape, shards, -0.22, 0.18) * entries
    return jnp.clip(entries, min=-bound, max=bound).astype(held_as)


def setup_inputs(seed: int = 0, part: int = 0) -> dict:
    splits = jax.random.split(jax.random.key(seed), 9)
    part_keys = jax.random.split(jax.random.fold_in(splits[8], part), 9)
    return {
        "pair": bell_draw(part_keys[0], (TOKENS, TOKENS, C), 1.0, 6.0, ((0, 4), (1, 4)), jnp.float32),
        "pair_mask": with_ends((jax.random.randint(part_keys[1], (TOKENS, TOKENS), 0, 8) < 7).astype(jnp.int32), jax.random.fold_in(part_keys[1], 1), 0, 1),
        "out_proj": bell_draw(splits[2], (C, 4 * H), C ** -0.5, 0.5, (), jnp.float32),
        "out_gate": bell_draw(splits[3], (C, C), C ** -0.5, 0.5, (), jnp.float32),
        "out_final": bell_draw(splits[4], (H, C), H ** -0.5, 0.5, (), jnp.float32),
        "in_proj": bell_draw(splits[5], (C, 4 * H), C ** -0.5, 0.5, (), jnp.float32),
        "in_gate": bell_draw(splits[6], (C, C), C ** -0.5, 0.5, (), jnp.float32),
        "in_final": bell_draw(splits[7], (H, C), H ** -0.5, 0.5, (), jnp.float32),
    }


def layer_norm(value):
    mean = lax.optimization_barrier(jnp.mean(value, axis=-1, keepdims=True))
    centred = value - mean
    variance = lax.optimization_barrier(jnp.mean(centred * centred, axis=-1, keepdims=True))
    return centred * lax.rsqrt(variance + 1e-05)

def project(pair, pair_mask, proj_weight, gate_weight):
    normed = layer_norm(pair)
    proj = jnp.einsum('ijc,cd->ijd', normed, proj_weight, precision=lax.Precision.HIGHEST)
    hidden = proj_weight.shape[1] // 4
    valid = pair_mask.astype(jnp.float32)[:, :, None]
    left = jax.nn.sigmoid(proj[..., :hidden]) * proj[..., hidden:2 * hidden] * valid
    right = jax.nn.sigmoid(proj[..., 2 * hidden:3 * hidden]) * proj[..., 3 * hidden:] * valid
    gate = jax.nn.sigmoid(jnp.einsum('ijc,cd->ijd', normed, gate_weight, precision=lax.Precision.HIGHEST))
    left = jnp.transpose(left.astype(jnp.bfloat16), (2, 0, 1))
    right = jnp.transpose(right.astype(jnp.bfloat16), (2, 0, 1))
    return (left, right, gate)

def finish(pair, summed, gate, final_weight):
    normed = layer_norm(jnp.transpose(summed, (1, 2, 0)))
    return pair + gate * jnp.einsum('ijh,hc->ijc', normed, final_weight, precision=lax.Precision.HIGHEST)

def reference(pair, pair_mask, out_proj, out_gate, out_final, in_proj, in_gate, in_final):
    width = pair.shape[0]
    hidden = out_final.shape[0]
    col_block = width // N_COL
    row_block = width // N_ROW
    left, right, gate = project(pair, pair_mask, out_proj, out_gate)
    left_blocks = jnp.transpose(left.reshape(hidden, width, N_COL, col_block), (2, 0, 1, 3))
    right_blocks = jnp.transpose(right.reshape(hidden, width, N_COL, col_block), (2, 0, 1, 3))

    def outer_step(total, pieces):
        part = jnp.einsum('hik,hjk->hij', pieces[0].astype(jnp.float32), pieces[1].astype(jnp.float32), precision=lax.Precision.HIGHEST)
        return (total + part.astype(jnp.bfloat16).astype(jnp.float32), None)
    outer, unused = lax.scan(outer_step, jnp.zeros((hidden, width, width), jnp.float32), (left_blocks, right_blocks))
    middle = finish(pair, outer, gate, out_final)
    left2, right2, gate2 = project(middle, pair_mask, in_proj, in_gate)
    left2_blocks = jnp.transpose(left2.reshape(hidden, N_ROW, row_block, width), (1, 0, 2, 3))
    right2_blocks = jnp.transpose(right2.reshape(hidden, N_ROW, row_block, width), (1, 0, 2, 3))

    def inner_step(total, pieces):
        part = jnp.einsum('hki,hkj->hij', pieces[0].astype(jnp.float32), pieces[1].astype(jnp.float32), precision=lax.Precision.HIGHEST)
        return (total + part.astype(jnp.bfloat16).astype(jnp.float32), None)
    inner, unused2 = lax.scan(inner_step, jnp.zeros((hidden, width, width), jnp.float32), (left2_blocks, right2_blocks))
    return finish(middle, inner, gate2, in_final)
```

```python
import jax
import jax.numpy as jnp
from jax import lax
from jax.experimental import pallas as pl
from jax.experimental.pallas import tpu as pltpu
from jax.sharding import PartitionSpec as P

MASKED = 64.0
SPLIT = 4
SIDE = 10
MAIN = 8
REST = SIDE - MAIN
ROWS = 112
WIDTH = SIDE * SPLIT


def layer_norm(value):
    mean = jnp.mean(value, axis=-1, keepdims=True)
    centred = value - mean
    variance = jnp.mean(centred * centred, axis=-1, keepdims=True)
    return centred * lax.rsqrt(variance + 1e-05)


def project(pair, pair_mask, proj_weight, gate_weight):
    normed = layer_norm(pair)
    proj = jnp.einsum("ijc,cd->ijd", normed, proj_weight, precision=lax.Precision.HIGHEST)
    hidden = proj_weight.shape[1] // 4
    valid = pair_mask.astype(jnp.float32)[:, :, None]
    left = jax.nn.sigmoid(proj[..., :hidden]) * proj[..., hidden : 2 * hidden] * valid
    right = jax.nn.sigmoid(proj[..., 2 * hidden : 3 * hidden]) * proj[..., 3 * hidden :] * valid
    gate = jax.nn.sigmoid(
        jnp.einsum("ijc,cd->ijd", normed, gate_weight, precision=lax.Precision.HIGHEST)
    )
    left = jnp.transpose(left.astype(jnp.bfloat16), (2, 0, 1))
    right = jnp.transpose(right.astype(jnp.bfloat16), (2, 0, 1))
    return (left, right, gate)


def finish(pair, summed, gate, final_weight):
    normed = layer_norm(jnp.transpose(summed, (1, 2, 0)))
    return pair + gate * jnp.einsum(
        "ijh,hc->ijc", normed, final_weight, precision=lax.Precision.HIGHEST
    )


def split_plan(pair, pair_mask, out_proj, out_gate, out_final, in_proj, in_gate, in_final):
    left, right, gate = project(pair, pair_mask, out_proj, out_gate)
    outer_terms = jnp.einsum(
        "hik,hjk->hij",
        left,
        lax.all_gather(right, "row", axis=1, tiled=True),
        preferred_element_type=jnp.float32,
    )
    outer = lax.psum_scatter(
        outer_terms.astype(jnp.bfloat16), "col", scatter_dimension=2, tiled=True
    ).astype(jnp.float32)
    middle = finish(pair, outer, gate, out_final)
    left2, right2, gate2 = project(middle, pair_mask, in_proj, in_gate)
    inner_terms = jnp.einsum(
        "hki,hkj->hij",
        lax.all_gather(left2, "col", axis=2, tiled=True),
        right2,
        preferred_element_type=jnp.float32,
    )
    inner = lax.psum_scatter(
        inner_terms.astype(jnp.bfloat16), "row", scatter_dimension=1, tiled=True
    ).astype(jnp.float32)
    return finish(middle, inner, gate2, in_final)


def sigmoid(value):
    return 0.5 * jnp.tanh(0.5 * value) + 0.5


def dot(value, weight):
    return jnp.dot(value.astype(jnp.bfloat16), weight, preferred_element_type=jnp.float32)


def scaled(centred):
    return centred * lax.rsqrt(jnp.mean(centred * centred, axis=-1, keepdims=True) + 1e-05)


def rest_rows(k):
    return 80 + 16 * k


def pack_kernel(pair_ref, mask_ref, tile_ref, own_ref, send_ref):
    own_ref[...] = jnp.zeros(own_ref.shape, own_ref.dtype)
    send_ref[...] = jnp.zeros(send_ref.shape, send_ref.dtype)
    valid = mask_ref[...]
    for k in range(SIDE):
        rows = pair_ref[:, k, :]
        centred = rows - jnp.mean(rows, axis=-1, keepdims=True)
        sent = jnp.where(valid[:, k : k + 1] > 0, centred, MASKED)
        own_ref[pl.ds(MAIN * k, MAIN), :] = rows[:MAIN]
        send_ref[pl.ds(MAIN * k, MAIN), :] = sent[:MAIN]
        for e in range(REST):
            own_ref[pl.ds(rest_rows(e) + k, 1), :] = rows[MAIN + e : MAIN + e + 1]
            send_ref[pl.ds(rest_rows(e) + k, 1), :] = sent[MAIN + e : MAIN + e + 1]
    tile_ref[...] = send_ref[...].astype(tile_ref.dtype)


def to_lines(target, base, tile, slot, slots, line):
    for k in range(SIDE):
        target[pl.ds(base + line * k + MAIN * slot, MAIN), :] = tile[MAIN * k : MAIN * (k + 1)]
    for e in range(REST):
        target[pl.ds(base + MAIN * slots + REST * slot + e, SIDE, stride=line), :] = tile[
            rest_rows(e) : rest_rows(e) + SIDE
        ]


def update_kernel(
    near_ref, far_ref, own_ref, out_proj_ref, out_gate_ref, out_final_ref, in_proj_ref, in_gate_ref, in_final_ref,
    result_ref,
    lines_ref, right_lines_ref, left_ref, right_ref, outer_ref, mid_ref, pieces_ref, flat_ref,
):
    bf16 = jnp.bfloat16
    row, col = lax.axis_index("row"), lax.axis_index("col")
    other = jnp.bitwise_xor(row, col)
    length = SIDE * WIDTH
    right_line = 24
    own = own_ref[...]
    own_centred = own - jnp.mean(own, axis=-1, keepdims=True)

    out_proj = out_proj_ref[...].astype(bf16)
    for part in range(SPLIT):
        source, place = (near_ref, far_ref)[part % 2], SPLIT * (part // 2)
        for slot in range(SPLIT):
            to_lines(lines_ref, part * length, source[place + slot].astype(jnp.float32), slot, SPLIT, WIDTH)
        to_lines(right_lines_ref, 0, source[place].astype(jnp.float32), 0, 2, right_line)
        to_lines(right_lines_ref, 0, source[place + other].astype(jnp.float32), 1, 2, right_line)
        raw = lines_ref[pl.ds(part * length, length), :]
        valid = raw < 0.5 * MASKED
        normed = scaled(jnp.where(valid, raw, 0.0))
        proj = dot(normed, out_proj[:, :256])
        left_ref[pl.ds(part * length, length), :] = sigmoid(proj[:, :128]) * proj[:, 128:]
        raw = right_lines_ref[...]
        normed = scaled(jnp.where(raw < 0.5 * MASKED, raw, 0.0))
        proj = dot(normed, out_proj[:, 256:])
        right_ref[pl.ds(part * SIDE * right_line, SIDE * right_line), :] = sigmoid(proj[:, :128]) * proj[:, 128:]

    group = 4

    def outer_step(g, carry):
        def add(k, sums):
            rows = left_ref[pl.ds(pl.multiple_of(k * WIDTH, 8), WIDTH), :]
            new = []
            for jj in range(group):
                one = right_ref[pl.ds(k * right_line + g * group + jj, 1), :]
                new.append(sums[jj] + rows * jnp.broadcast_to(one, rows.shape))
            return tuple(new)

        sums = lax.fori_loop(
            0, WIDTH, add, tuple(jnp.zeros((WIDTH, 128), jnp.float32) for _ in range(group)), unroll=4
        )
        for jj in range(group):
            outer_ref[pl.ds(pl.multiple_of((g * group + jj) * WIDTH, 8), WIDTH), :] = sums[jj]
        return carry

    lax.fori_loop(0, 2 * SIDE // group, outer_step, 0)

    out_gate = out_gate_ref[...].astype(bf16)
    out_final = out_final_ref[...].astype(bf16)
    in_proj = in_proj_ref[...].astype(bf16)
    for block in range(2):
        start = pl.multiple_of(other * length, 8) if block == 1 else 0
        raw = lines_ref[pl.ds(start, length), :]
        valid = raw < 0.5 * MASKED
        centred = jnp.where(valid, raw, 0.0)
        if block == 0:
            mid_ref[pl.ds(0, length), :] = centred
            for k in range(SIDE):
                mid_ref[pl.ds(WIDTH * k, MAIN), :] = own_centred[MAIN * k : MAIN * (k + 1)]
            for e in range(REST):
                mid_ref[pl.ds(MAIN * SPLIT + e, SIDE, stride=WIDTH), :] = own_centred[rest_rows(e) : rest_rows(e) + SIDE]
            centred = mid_ref[pl.ds(0, length), :]
        gate = sigmoid(dot(scaled(centred), out_gate))
        from_slot = 1 - block
        summed = jnp.concatenate(
            [outer_ref[pl.ds(from_slot * MAIN * WIDTH, MAIN * WIDTH), :],
             outer_ref[pl.ds((2 * MAIN + REST * from_slot) * WIDTH, REST * WIDTH), :]], axis=0)
        change = gate * dot(layer_norm(summed), out_final)
        mid = centred + change
        normed = layer_norm(mid)
        proj = dot(normed, in_proj[:, 256:] if block == 0 else in_proj[:, :256])
        value = jnp.where(valid, sigmoid(proj[:, :128]) * proj[:, 128:], 0.0)
        if block == 0:
            right_ref[pl.ds(0, length), :] = value
            mid_ref[pl.ds(0, length), :] = change
            mid_ref[pl.ds(length, length), :] = normed
        else:
            left_ref[pl.ds(0, length), :] = value

    def inner_step(j, carry):
        right = right_ref[pl.ds(pl.multiple_of(j * WIDTH, 8), WIDTH), :]
        for i in range(SIDE):
            product = left_ref[pl.ds(i * WIDTH, WIDTH), :] * right
            folded = product[:8]
            for t in range(1, WIDTH // 8):
                folded = folded + product[8 * t : 8 * (t + 1)]
            at = MAIN * j + i if i < MAIN else rest_rows(i - MAIN) + j
            pieces_ref[pl.ds(pl.multiple_of(8 * at, 8), 8), :] = folded
        return carry

    lax.fori_loop(0, SIDE, inner_step, 0)
    inner = pieces_ref[pl.ds(0, ROWS, stride=8), :]
    for t in range(1, 8):
        inner = inner + pieces_ref[pl.ds(t, ROWS, stride=8), :]

    def own_rows(base):
        for k in range(SIDE):
            flat_ref[pl.ds(MAIN * k, MAIN), :] = mid_ref[pl.ds(base + WIDTH * k, MAIN), :]
        for e in range(REST):
            flat_ref[pl.ds(rest_rows(e), SIDE), :] = mid_ref[pl.ds(base + MAIN * SPLIT + e, SIDE, stride=WIDTH), :]
        return flat_ref[...]

    mid = own + own_rows(0)
    gate = sigmoid(dot(own_rows(length), in_gate_ref[...].astype(bf16)))
    result = mid + gate * dot(layer_norm(inner), in_final_ref[...].astype(bf16))
    for k in range(SIDE):
        result_ref[pl.ds(0, MAIN), k, :] = result[MAIN * k : MAIN * (k + 1)]
        for e in range(REST):
            result_ref[MAIN + e, pl.ds(k, 1), :] = result[rest_rows(e) + k : rest_rows(e) + k + 1]


def swapped(value, rows, cols):
    pairs = [
        (r * SPLIT + c, (r ^ rows) * SPLIT + (c ^ cols)) for r in range(SPLIT) for c in range(SPLIT)
    ]
    return lax.ppermute(value, ("row", "col"), pairs)


def in_vmem(value):
    return pltpu.with_memory_space_constraint(value, pltpu.VMEM)


def compact_plan(pair, pair_mask, out_proj, out_gate, out_final, in_proj, in_gate, in_final):
    f32 = jnp.float32
    tile, own = pl.pallas_call(
        pack_kernel,
        out_shape=(pltpu.VMEM((ROWS, 128), jnp.bfloat16), pltpu.VMEM((ROWS, 128), f32)),
        scratch_shapes=[pltpu.VMEM((ROWS, 128), f32)],
        name="pack",
    )(pair, pair_mask)
    along_row = [swapped(tile, s, 0) for s in (3, 2, 1)]
    column = jnp.stack([tile] + along_row[::-1])
    near = jnp.concatenate([column, swapped(column, 0, 2)])
    far = swapped(near, 0, 1)
    length = SIDE * WIDTH
    return pl.pallas_call(
        update_kernel,
        out_shape=jax.ShapeDtypeStruct(pair.shape, f32),
        scratch_shapes=[
            pltpu.VMEM((SPLIT * length, 128), f32),
            pltpu.VMEM((SIDE * 24, 128), f32),
            pltpu.VMEM((SPLIT * length, 128), f32),
            pltpu.VMEM((SPLIT * SIDE * 24, 128), f32),
            pltpu.VMEM((2 * length, 128), f32),
            pltpu.VMEM((2 * length, 128), f32),
            pltpu.VMEM((8 * ROWS, 128), f32),
            pltpu.VMEM((ROWS, 128), f32),
        ],
        compiler_params=pltpu.CompilerParams(vmem_limit_bytes=32 << 20),
        name="update",
    )(in_vmem(near), in_vmem(far), in_vmem(own), *map(in_vmem, (out_proj, out_gate, out_final, in_proj, in_gate, in_final)))


def solution(mesh):
    def body(pair, *rest):
        compact = (
            mesh.shape["row"] == mesh.shape["col"] == SPLIT
            and pair.shape == (SIDE, SIDE, 128)
            and rest[1].shape == (128, 512)
        )
        return (compact_plan if compact else split_plan)(pair, *rest)

    return jax.shard_map(
        body,
        mesh=mesh,
        in_specs=(
            P(("grp", "row"), "col", None),
            P(("grp", "row"), "col"),
            P(),
            P(),
            P(),
            P(),
            P(),
            P(),
        ),
        out_specs=P(("grp", "row"), "col", None),
        check_vma=False,
    )
```

```python
import jax
import jax.numpy as jnp
from jax import lax
from jax.experimental import pallas as pl
from jax.experimental.pallas import tpu as pltpu
from jax.sharding import PartitionSpec as P

MASKED = 64.0
SPLIT = 4
SIDE = 10
MAIN = 8
REST = SIDE - MAIN
ROWS = 112
WIDTH = SIDE * SPLIT


def layer_norm(value):
    mean = jnp.mean(value, axis=-1, keepdims=True)
    centred = value - mean
    variance = jnp.mean(centred * centred, axis=-1, keepdims=True)
    return centred * lax.rsqrt(variance + 1e-05)


def project(pair, pair_mask, proj_weight, gate_weight):
    normed = layer_norm(pair)
    proj = jnp.einsum("ijc,cd->ijd", normed, proj_weight, precision=lax.Precision.HIGHEST)
    hidden = proj_weight.shape[1] // 4
    valid = pair_mask.astype(jnp.float32)[:, :, None]
    left = jax.nn.sigmoid(proj[..., :hidden]) * proj[..., hidden : 2 * hidden] * valid
    right = jax.nn.sigmoid(proj[..., 2 * hidden : 3 * hidden]) * proj[..., 3 * hidden :] * valid
    gate = jax.nn.sigmoid(
        jnp.einsum("ijc,cd->ijd", normed, gate_weight, precision=lax.Precision.HIGHEST)
    )
    left = jnp.transpose(left.astype(jnp.bfloat16), (2, 0, 1))
    right = jnp.transpose(right.astype(jnp.bfloat16), (2, 0, 1))
    return (left, right, gate)


def finish(pair, summed, gate, final_weight):
    normed = layer_norm(jnp.transpose(summed, (1, 2, 0)))
    return pair + gate * jnp.einsum(
        "ijh,hc->ijc", normed, final_weight, precision=lax.Precision.HIGHEST
    )


def split_plan(pair, pair_mask, out_proj, out_gate, out_final, in_proj, in_gate, in_final):
    left, right, gate = project(pair, pair_mask, out_proj, out_gate)
    outer_terms = jnp.einsum(
        "hik,hjk->hij",
        left,
        lax.all_gather(right, "row", axis=1, tiled=True),
        preferred_element_type=jnp.float32,
    )
    outer = lax.psum_scatter(
        outer_terms.astype(jnp.bfloat16), "col", scatter_dimension=2, tiled=True
    ).astype(jnp.float32)
    middle = finish(pair, outer, gate, out_final)
    left2, right2, gate2 = project(middle, pair_mask, in_proj, in_gate)
    inner_terms = jnp.einsum(
        "hki,hkj->hij",
        lax.all_gather(left2, "col", axis=2, tiled=True),
        right2,
        preferred_element_type=jnp.float32,
    )
    inner = lax.psum_scatter(
        inner_terms.astype(jnp.bfloat16), "row", scatter_dimension=1, tiled=True
    ).astype(jnp.float32)
    return finish(middle, inner, gate2, in_final)


def sigmoid(value):
    return 0.5 * jnp.tanh(0.5 * value) + 0.5


def dot(value, weight):
    return jnp.dot(value.astype(jnp.bfloat16), weight, preferred_element_type=jnp.float32)


def scaled(centred):
    return centred * lax.rsqrt(jnp.mean(centred * centred, axis=-1, keepdims=True) + 1e-05)


def rest_rows(k):
    return 80 + 16 * k


def pack_kernel(pair_ref, mask_ref, tile_ref, own_ref, send_ref):
    own_ref[...] = jnp.zeros(own_ref.shape, own_ref.dtype)
    send_ref[...] = jnp.zeros(send_ref.shape, send_ref.dtype)
    valid = mask_ref[...]
    for k in range(SIDE):
        rows = pair_ref[:, k, :]
        centred = rows - jnp.mean(rows, axis=-1, keepdims=True)
        sent = jnp.where(valid[:, k : k + 1] > 0, centred, MASKED)
        own_ref[pl.ds(MAIN * k, MAIN), :] = rows[:MAIN]
        send_ref[pl.ds(MAIN * k, MAIN), :] = sent[:MAIN]
        for e in range(REST):
            own_ref[pl.ds(rest_rows(e) + k, 1), :] = rows[MAIN + e : MAIN + e + 1]
            send_ref[pl.ds(rest_rows(e) + k, 1), :] = sent[MAIN + e : MAIN + e + 1]
    tile_ref[...] = send_ref[...].astype(tile_ref.dtype)


def to_lines(target, base, tile, slot, slots, line):
    for k in range(SIDE):
        target[pl.ds(base + line * k + MAIN * slot, MAIN), :] = tile[MAIN * k : MAIN * (k + 1)]
    for e in range(REST):
        target[pl.ds(base + MAIN * slots + REST * slot + e, SIDE, stride=line), :] = tile[
            rest_rows(e) : rest_rows(e) + SIDE
        ]


RIGHT_LINE = 24
LENGTH = SIDE * WIDTH
GROUP = 4


def add_terms(tiles, other, out_proj, first, outer_ref, lines_ref, right_lines_ref, left_ref, right_ref):
    for slot in range(SPLIT):
        to_lines(lines_ref, 0, tiles[slot].astype(jnp.float32), slot, SPLIT, WIDTH)
    to_lines(right_lines_ref, 0, tiles[0].astype(jnp.float32), 0, 2, RIGHT_LINE)
    to_lines(right_lines_ref, 0, tiles[other].astype(jnp.float32), 1, 2, RIGHT_LINE)
    for raw_ref, weight, value_ref in (
        (lines_ref, out_proj[:, :256], left_ref),
        (right_lines_ref, out_proj[:, 256:], right_ref),
    ):
        raw = raw_ref[...]
        proj = dot(scaled(jnp.where(raw < 0.5 * MASKED, raw, 0.0)), weight)
        value_ref[...] = sigmoid(proj[:, :128]) * proj[:, 128:]

    def step(g, carry):
        at = [pl.ds(pl.multiple_of((g * GROUP + t) * WIDTH, 8), WIDTH) for t in range(GROUP)]
        sums = [jnp.zeros((WIDTH, 128), jnp.float32) if first else outer_ref[at[t], :] for t in range(GROUP)]
        for k in range(SIDE):
            rows = left_ref[pl.ds(k * WIDTH, WIDTH), :]
            for t in range(GROUP):
                one = right_ref[pl.ds(k * RIGHT_LINE + g * GROUP + t, 1), :]
                sums[t] = sums[t] + rows * jnp.broadcast_to(one, rows.shape)
        for t in range(GROUP):
            outer_ref[at[t], :] = sums[t]
        return carry

    lax.fori_loop(0, 2 * SIDE // GROUP, step, 0)


def split_lines(raw):
    valid = raw < 0.5 * MASKED
    return jnp.where(valid, raw, 0.0), valid


def other_slot():
    before = lax.rem(lax.axis_index("row") - lax.axis_index("col") + SPLIT, SPLIT)
    place = jnp.int32(0)
    for number, step in enumerate(STEPS):
        place = jnp.where(before == step, number + 1, place)
    return place


def other_part():
    return jnp.bitwise_xor(lax.axis_index("row"), lax.axis_index("col"))


def first_kernel(
    tiles, own_ref, out_proj_ref, out_gate_ref, outer_ref, centred_ref, gate_ref, valid_ref, *scratch
):
    lines_ref = scratch[0]
    add_terms(tiles, other_slot(), out_proj_ref[...].astype(jnp.bfloat16), True, outer_ref, *scratch)
    centred, valid = split_lines(lines_ref[...])
    centred_ref[...] = centred
    valid_ref[...] = jnp.where(valid, 1.0, 0.0)
    own = own_ref[...]
    own = own - jnp.mean(own, axis=-1, keepdims=True)
    to_lines(centred_ref, 0, own, 0, SPLIT, WIDTH)
    gate_ref[...] = sigmoid(dot(scaled(centred_ref[...]), out_gate_ref[...].astype(jnp.bfloat16)))


def next_kernel(tiles, out_proj_ref, before_ref, outer_ref, *scratch):
    outer_ref[...] = before_ref[...]
    add_terms(tiles, other_slot(), out_proj_ref[...].astype(jnp.bfloat16), False, outer_ref, *scratch)


def last_kernel(
    part0, part1, part2, part3, before_ref, centred0_ref, gate0_ref, valid0_ref, own_ref,
    out_proj_ref, out_gate_ref, out_final_ref, in_proj_ref, in_gate_ref, in_final_ref,
    result_ref,
    lines_ref, right_lines_ref, left_ref, right_ref, outer_ref, mid_ref, pieces_ref, flat_ref,
):
    bf16 = jnp.bfloat16
    other = other_slot()
    outer_ref[...] = before_ref[...]
    add_terms(
        part3, other, out_proj_ref[...].astype(bf16), False, outer_ref,
        lines_ref, right_lines_ref, left_ref, right_ref.at[pl.ds(0, SIDE * RIGHT_LINE)],
    )
    for number, tiles in enumerate((part0, part1, part2, part3)):
        @pl.when(other_part() == number)
        def _():
            for slot in range(SPLIT):
                to_lines(lines_ref, 0, tiles[slot].astype(jnp.float32), slot, SPLIT, WIDTH)

    out_final = out_final_ref[...].astype(bf16)
    in_proj = in_proj_ref[...].astype(bf16)
    for block in range(2):
        if block == 0:
            centred, gate, valid = centred0_ref[...], gate0_ref[...], valid0_ref[...] > 0.5
        else:
            centred, valid = split_lines(lines_ref[...])
            gate = sigmoid(dot(scaled(centred), out_gate_ref[...].astype(bf16)))
        slot = 1 - block
        summed = jnp.concatenate(
            [
                outer_ref[pl.ds(slot * MAIN * WIDTH, MAIN * WIDTH), :],
                outer_ref[pl.ds((2 * MAIN + REST * slot) * WIDTH, REST * WIDTH), :],
            ],
            axis=0,
        )
        change = gate * dot(layer_norm(summed), out_final)
        normed = layer_norm(centred + change)
        proj = dot(normed, in_proj[:, 256:] if block == 0 else in_proj[:, :256])
        value = jnp.where(valid, sigmoid(proj[:, :128]) * proj[:, 128:], 0.0)
        if block == 0:
            right_ref[...] = value
            mid_ref[pl.ds(0, LENGTH), :] = change
            mid_ref[pl.ds(LENGTH, LENGTH), :] = normed
        else:
            left_ref[...] = value

    def inner_step(j, carry):
        right = right_ref[pl.ds(pl.multiple_of(j * WIDTH, 8), WIDTH), :]
        for i in range(SIDE):
            product = left_ref[pl.ds(i * WIDTH, WIDTH), :] * right
            folded = product[:8]
            for t in range(1, WIDTH // 8):
                folded = folded + product[8 * t : 8 * (t + 1)]
            at = MAIN * j + i if i < MAIN else rest_rows(i - MAIN) + j
            pieces_ref[pl.ds(pl.multiple_of(8 * at, 8), 8), :] = folded
        return carry

    lax.fori_loop(0, SIDE, inner_step, 0)
    inner = pieces_ref[pl.ds(0, ROWS, stride=8), :]
    for t in range(1, 8):
        inner = inner + pieces_ref[pl.ds(t, ROWS, stride=8), :]

    def own_rows(base):
        for k in range(SIDE):
            flat_ref[pl.ds(MAIN * k, MAIN), :] = mid_ref[pl.ds(base + WIDTH * k, MAIN), :]
        for e in range(REST):
            flat_ref[pl.ds(rest_rows(e), SIDE), :] = mid_ref[pl.ds(base + MAIN * SPLIT + e, SIDE, stride=WIDTH), :]
        return flat_ref[...]

    mid = own_ref[...] + own_rows(0)
    gate = sigmoid(dot(own_rows(LENGTH), in_gate_ref[...].astype(bf16)))
    result = mid + gate * dot(layer_norm(inner), in_final_ref[...].astype(bf16))
    for k in range(SIDE):
        result_ref[pl.ds(0, MAIN), k, :] = result[MAIN * k : MAIN * (k + 1)]
        for e in range(REST):
            result_ref[MAIN + e, pl.ds(k, 1), :] = result[rest_rows(e) + k : rest_rows(e) + k + 1]


def swapped(value, rows, cols):
    pairs = [
        (r * SPLIT + c, (r ^ rows) * SPLIT + (c ^ cols)) for r in range(SPLIT) for c in range(SPLIT)
    ]
    return lax.ppermute(value, ("row", "col"), pairs)


STEPS = (1, 3, 2)


def shifted(value, step):
    pairs = [
        (r * SPLIT + c, (r + step) % SPLIT * SPLIT + c) for r in range(SPLIT) for c in range(SPLIT)
    ]
    return lax.ppermute(value, ("row", "col"), pairs)


def in_vmem(value):
    return pltpu.with_memory_space_constraint(value, pltpu.VMEM)


def call(kernel, name, cycles, out, scratch, *operands, grant=32 << 20):
    return pl.pallas_call(
        kernel,
        out_shape=out,
        scratch_shapes=[pltpu.VMEM(shape, jnp.float32) for shape in scratch],
        cost_estimate=pl.CostEstimate(flops=cycles, bytes_accessed=0, transcendentals=0),
        compiler_params=pltpu.CompilerParams(vmem_limit_bytes=grant),
        name=name,
    )(*operands)


def compact_plan(pair, pair_mask, *weights):
    f32 = jnp.float32
    out_proj, out_gate, out_final, in_proj, in_gate, in_final = map(in_vmem, weights)
    tile, own = call(
        pack_kernel, "pack", 1000, (pltpu.VMEM((ROWS, 128), jnp.bfloat16), pltpu.VMEM((ROWS, 128), f32)),
        [(ROWS, 128)], pair, pair_mask, grant=None,
    )
    around = [tile] + [shifted(tile, step) for step in STEPS]
    early = jnp.stack(around[:2])
    swapped_early = swapped(early, 0, 2)
    two, three, _ = lax.optimization_barrier((around[2], around[3], early))
    late = jnp.stack([two, three])
    part0 = jnp.concatenate([early, late])
    part2 = jnp.concatenate([swapped_early, swapped(late, 0, 2)])
    lines = pltpu.VMEM((LENGTH, 128), f32)
    sums = pltpu.VMEM((2 * LENGTH, 128), f32)
    work = [(LENGTH, 128), (SIDE * RIGHT_LINE, 128), (LENGTH, 128), (SIDE * RIGHT_LINE, 128)]
    cost = 1 << 10
    outer, centred0, gate0, valid0 = call(
        first_kernel, "first", cost, (sums, lines, lines, lines), work, in_vmem(part0), in_vmem(own), out_proj, out_gate
    )
    part2, outer = lax.optimization_barrier((part2, outer))
    part1 = swapped(part0, 0, 1)
    outer = call(next_kernel, "second", cost, sums, work, in_vmem(part1), out_proj, in_vmem(outer))
    part3 = swapped(part2, 0, 1)
    outer = call(next_kernel, "third", cost, sums, work, in_vmem(part2), out_proj, in_vmem(outer))
    part3, outer = lax.optimization_barrier((part3, outer))
    return call(
        last_kernel, "last", cost, jax.ShapeDtypeStruct(pair.shape, f32),
        work[:3] + [(LENGTH, 128), (2 * LENGTH, 128), (2 * LENGTH, 128), (8 * ROWS, 128), (ROWS, 128)],
        *map(in_vmem, (part0, part1, part2, part3, outer, centred0, gate0, valid0, own)),
        out_proj, out_gate, out_final, in_proj, in_gate, in_final,
    )


def solution(mesh):
    def body(pair, *rest):
        compact = (
            mesh.shape["row"] == mesh.shape["col"] == SPLIT
            and pair.shape == (SIDE, SIDE, 128)
            and rest[1].shape == (128, 512)
        )
        return (compact_plan if compact else split_plan)(pair, *rest)

    return jax.shard_map(
        body,
        mesh=mesh,
        in_specs=(
            P(("grp", "row"), "col", None),
            P(("grp", "row"), "col"),
            P(),
            P(),
            P(),
            P(),
            P(),
            P(),
        ),
        out_specs=P(("grp", "row"), "col", None),
        check_vma=False,
    )
```

```python
import jax
import jax.numpy as jnp
from jax import lax
from jax.experimental import pallas as pl
from jax.experimental.pallas import tpu as pltpu
from jax.sharding import PartitionSpec as P

MASKED = 64.0
SPLIT = 4
SIDE = 10
MAIN = 8
REST = SIDE - MAIN
ROWS = 112
WIDTH = SIDE * SPLIT


def layer_norm(value):
    mean = jnp.mean(value, axis=-1, keepdims=True)
    centred = value - mean
    variance = jnp.mean(centred * centred, axis=-1, keepdims=True)
    return centred * lax.rsqrt(variance + 1e-05)


def project(pair, pair_mask, proj_weight, gate_weight):
    normed = layer_norm(pair)
    proj = jnp.einsum("ijc,cd->ijd", normed, proj_weight, precision=lax.Precision.HIGHEST)
    hidden = proj_weight.shape[1] // 4
    valid = pair_mask.astype(jnp.float32)[:, :, None]
    left = jax.nn.sigmoid(proj[..., :hidden]) * proj[..., hidden : 2 * hidden] * valid
    right = jax.nn.sigmoid(proj[..., 2 * hidden : 3 * hidden]) * proj[..., 3 * hidden :] * valid
    gate = jax.nn.sigmoid(
        jnp.einsum("ijc,cd->ijd", normed, gate_weight, precision=lax.Precision.HIGHEST)
    )
    left = jnp.transpose(left.astype(jnp.bfloat16), (2, 0, 1))
    right = jnp.transpose(right.astype(jnp.bfloat16), (2, 0, 1))
    return (left, right, gate)


def finish(pair, summed, gate, final_weight):
    normed = layer_norm(jnp.transpose(summed, (1, 2, 0)))
    return pair + gate * jnp.einsum(
        "ijh,hc->ijc", normed, final_weight, precision=lax.Precision.HIGHEST
    )


def split_plan(pair, pair_mask, out_proj, out_gate, out_final, in_proj, in_gate, in_final):
    left, right, gate = project(pair, pair_mask, out_proj, out_gate)
    outer_terms = jnp.einsum(
        "hik,hjk->hij",
        left,
        lax.all_gather(right, "row", axis=1, tiled=True),
        preferred_element_type=jnp.float32,
    )
    outer = lax.psum_scatter(
        outer_terms.astype(jnp.bfloat16), "col", scatter_dimension=2, tiled=True
    ).astype(jnp.float32)
    middle = finish(pair, outer, gate, out_final)
    left2, right2, gate2 = project(middle, pair_mask, in_proj, in_gate)
    inner_terms = jnp.einsum(
        "hki,hkj->hij",
        lax.all_gather(left2, "col", axis=2, tiled=True),
        right2,
        preferred_element_type=jnp.float32,
    )
    inner = lax.psum_scatter(
        inner_terms.astype(jnp.bfloat16), "row", scatter_dimension=1, tiled=True
    ).astype(jnp.float32)
    return finish(middle, inner, gate2, in_final)


def sigmoid(value):
    return 0.5 * jnp.tanh(0.5 * value) + 0.5


def dot(value, weight):
    return jnp.dot(value.astype(jnp.bfloat16), weight, preferred_element_type=jnp.float32)


def scaled(centred):
    return centred * lax.rsqrt(jnp.mean(centred * centred, axis=-1, keepdims=True) + 1e-05)


def rest_rows(k):
    return 80 + 16 * k


def pack_kernel(pair_ref, mask_ref, tile_ref, own_ref, send_ref):
    own_ref[...] = jnp.zeros(own_ref.shape, own_ref.dtype)
    send_ref[...] = jnp.zeros(send_ref.shape, send_ref.dtype)
    valid = mask_ref[...]
    for k in range(SIDE):
        rows = pair_ref[:, k, :]
        centred = rows - jnp.mean(rows, axis=-1, keepdims=True)
        sent = jnp.where(valid[:, k : k + 1] > 0, centred, MASKED)
        own_ref[pl.ds(MAIN * k, MAIN), :] = rows[:MAIN]
        send_ref[pl.ds(MAIN * k, MAIN), :] = sent[:MAIN]
        for e in range(REST):
            own_ref[pl.ds(rest_rows(e) + k, 1), :] = rows[MAIN + e : MAIN + e + 1]
            send_ref[pl.ds(rest_rows(e) + k, 1), :] = sent[MAIN + e : MAIN + e + 1]
    tile_ref[...] = send_ref[...].astype(tile_ref.dtype)


OUT_PROJ, OUT_GATE, OUT_FINAL, IN_PROJ, IN_GATE, IN_FINAL, WEIGHTS = 0, 512, 640, 768, 1280, 1408, 1536


def weights_kernel(*refs):
    start = 0
    for weight_ref in refs[:-1]:
        width = weight_ref.shape[1]
        refs[-1][:, pl.ds(start, width)] = weight_ref[...].astype(refs[-1].dtype)
        start += width


def to_lines(target, base, tile, slot, slots, line):
    for k in range(SIDE):
        target[pl.ds(base + line * k + MAIN * slot, MAIN), :] = tile[MAIN * k : MAIN * (k + 1)]
    for e in range(REST):
        target[pl.ds(base + MAIN * slots + REST * slot + e, SIDE, stride=line), :] = tile[
            rest_rows(e) : rest_rows(e) + SIDE
        ]


RIGHT_LINE = 24
LENGTH = SIDE * WIDTH
GROUP = 4


def add_terms(tiles, other, weights_ref, before_ref, outer_ref, lines_ref, right_lines_ref, left_ref, right_ref):
    for slot in range(SPLIT):
        to_lines(lines_ref, 0, tiles[slot].astype(jnp.float32), slot, SPLIT, WIDTH)
    to_lines(right_lines_ref, 0, tiles[0].astype(jnp.float32), 0, 2, RIGHT_LINE)
    to_lines(right_lines_ref, 0, tiles[other].astype(jnp.float32), 1, 2, RIGHT_LINE)
    raw = jnp.concatenate([lines_ref[...], right_lines_ref[...]], axis=0)
    normed = scaled(split_lines(raw)[0])
    proj = dot(normed[:LENGTH], weights_ref[:, pl.ds(OUT_PROJ, 256)])
    left_ref[...] = sigmoid(proj[:, :128]) * proj[:, 128:]
    proj = dot(normed[LENGTH:], weights_ref[:, pl.ds(OUT_PROJ + 256, 256)])
    right_ref[...] = sigmoid(proj[:, :128]) * proj[:, 128:]

    for g in range(2 * SIDE // GROUP):
        at = [pl.ds((g * GROUP + t) * WIDTH, WIDTH) for t in range(GROUP)]
        sums = [None if before_ref is None else before_ref[at[t], :] for t in range(GROUP)]
        for k in range(SIDE):
            rows = left_ref[pl.ds(k * WIDTH, WIDTH), :]
            for t in range(GROUP):
                one = right_ref[pl.ds(k * RIGHT_LINE + g * GROUP + t, 1), :]
                term = rows * jnp.broadcast_to(one, rows.shape)
                sums[t] = term if sums[t] is None else sums[t] + term
        for t in range(GROUP):
            outer_ref[at[t], :] = sums[t]


def split_lines(raw):
    valid = raw < 0.5 * MASKED
    return jnp.where(valid, raw, 0.0), valid


def other_slot():
    before = lax.rem(lax.axis_index("row") - lax.axis_index("col") + SPLIT, SPLIT)
    place = jnp.int32(0)
    for number, step in enumerate(STEPS):
        place = jnp.where(before == step, number + 1, place)
    return place


def other_part():
    return jnp.bitwise_xor(lax.axis_index("row"), lax.axis_index("col"))


def first_kernel(
    tiles, own_ref, weights_ref, outer_ref, centred_ref, gate_ref, valid_ref, *scratch
):
    lines_ref = scratch[0]
    add_terms(tiles, other_slot(), weights_ref, None, outer_ref, *scratch)
    centred, valid = split_lines(lines_ref[...])
    centred_ref[...] = centred
    valid_ref[...] = jnp.where(valid, 1.0, 0.0)
    own = own_ref[...]
    own = own - jnp.mean(own, axis=-1, keepdims=True)
    to_lines(centred_ref, 0, own, 0, SPLIT, WIDTH)
    gate_ref[...] = sigmoid(dot(scaled(centred_ref[...]), weights_ref[:, pl.ds(OUT_GATE, 128)]))


def next_kernel(tiles, weights_ref, before_ref, outer_ref, *scratch):
    add_terms(tiles, other_slot(), weights_ref, before_ref, outer_ref, *scratch)


def last_kernel(
    part0, part1, part2, part3, before_ref, centred0_ref, gate0_ref, valid0_ref, own_ref,
    weights_ref,
    result_ref,
    lines_ref, right_lines_ref, left_ref, right_ref, outer_ref, block_ref, left2_ref, right2_ref, mid_ref, normed_ref,
    pieces_ref, flat_ref, flat2_ref,
):
    for number, tiles in enumerate((part0, part1, part2, part3)):
        @pl.when(other_part() == number)
        def _():
            for slot in range(SPLIT):
                to_lines(block_ref, 0, tiles[slot].astype(jnp.float32), slot, SPLIT, WIDTH)

    add_terms(
        part3, other_slot(), weights_ref, before_ref, outer_ref,
        lines_ref, right_lines_ref, left_ref, right_ref,
    )

    def sums_of(slot):
        return [
            outer_ref[pl.ds(slot * MAIN * WIDTH, MAIN * WIDTH), :],
            outer_ref[pl.ds((2 * MAIN + REST * slot) * WIDTH, REST * WIDTH), :],
        ]

    centred1, valid1 = split_lines(block_ref[...])
    gate1 = sigmoid(dot(scaled(centred1), weights_ref[:, pl.ds(OUT_GATE, 128)]))
    gate = jnp.concatenate([gate0_ref[...], gate1], axis=0)
    centred = jnp.concatenate([centred0_ref[...], centred1], axis=0)
    change = gate * dot(layer_norm(jnp.concatenate(sums_of(1) + sums_of(0), axis=0)), weights_ref[:, pl.ds(OUT_FINAL, 128)])
    normed = layer_norm(centred + change)
    mid_ref[...] = change[:LENGTH]
    normed_ref[...] = normed[:LENGTH]
    proj = dot(normed[:LENGTH], weights_ref[:, pl.ds(IN_PROJ + 256, 256)])
    right2_ref[...] = jnp.where(valid0_ref[...] > 0.5, sigmoid(proj[:, :128]) * proj[:, 128:], 0.0)
    proj = dot(normed[LENGTH:], weights_ref[:, pl.ds(IN_PROJ, 256)])
    left2_ref[...] = jnp.where(valid1, sigmoid(proj[:, :128]) * proj[:, 128:], 0.0)

    for j in range(SIDE):
        right = right2_ref[pl.ds(j * WIDTH, WIDTH), :]
        for i in range(SIDE):
            product = left2_ref[pl.ds(i * WIDTH, WIDTH), :] * right
            folded = product[:8]
            for t in range(1, WIDTH // 8):
                folded = folded + product[8 * t : 8 * (t + 1)]
            at = MAIN * j + i if i < MAIN else rest_rows(i - MAIN) + j
            pieces_ref[pl.ds(8 * at, 8), :] = folded
    inner = pieces_ref[pl.ds(0, ROWS, stride=8), :]
    for t in range(1, 8):
        inner = inner + pieces_ref[pl.ds(t, ROWS, stride=8), :]

    def own_rows(source_ref, flat_ref):
        for k in range(SIDE):
            flat_ref[pl.ds(MAIN * k, MAIN), :] = source_ref[pl.ds(WIDTH * k, MAIN), :]
        for e in range(REST):
            flat_ref[pl.ds(rest_rows(e), SIDE), :] = source_ref[pl.ds(MAIN * SPLIT + e, SIDE, stride=WIDTH), :]
        return flat_ref[...]

    mid = own_ref[...] + own_rows(mid_ref, flat_ref)
    gate = sigmoid(dot(own_rows(normed_ref, flat2_ref), weights_ref[:, pl.ds(IN_GATE, 128)]))
    result = mid + gate * dot(layer_norm(inner), weights_ref[:, pl.ds(IN_FINAL, 128)])
    for k in range(SIDE):
        result_ref[pl.ds(0, MAIN), k, :] = result[MAIN * k : MAIN * (k + 1)]
        for e in range(REST):
            result_ref[MAIN + e, pl.ds(k, 1), :] = result[rest_rows(e) + k : rest_rows(e) + k + 1]


def swapped(value, rows, cols):
    pairs = [
        (r * SPLIT + c, (r ^ rows) * SPLIT + (c ^ cols)) for r in range(SPLIT) for c in range(SPLIT)
    ]
    return lax.ppermute(value, ("row", "col"), pairs)


STEPS = (2, 1, 3)


def shifted(value, step):
    pairs = [
        (r * SPLIT + c, (r + step) % SPLIT * SPLIT + c) for r in range(SPLIT) for c in range(SPLIT)
    ]
    return lax.ppermute(value, ("row", "col"), pairs)


def in_vmem(value):
    return pltpu.with_memory_space_constraint(value, pltpu.VMEM)


def call(kernel, name, cycles, out, scratch, *operands, grant=32 << 20):
    return pl.pallas_call(
        kernel,
        out_shape=out,
        scratch_shapes=[pltpu.VMEM(shape, jnp.float32) for shape in scratch],
        cost_estimate=pl.CostEstimate(flops=cycles, bytes_accessed=0, transcendentals=0),
        compiler_params=pltpu.CompilerParams(vmem_limit_bytes=grant),
        name=name,
    )(*operands)


def compact_plan(pair, pair_mask, *weights):
    f32 = jnp.float32
    tile, own = call(
        pack_kernel, "pack", 1000, (pltpu.VMEM((ROWS, 128), jnp.bfloat16), pltpu.VMEM((ROWS, 128), f32)),
        [(ROWS, 128)], pair, pair_mask, grant=None,
    )
    weights = call(
        weights_kernel, "weights", 1000, pltpu.VMEM((128, WEIGHTS), jnp.bfloat16), [], *weights, grant=None
    )
    around = [tile] + [shifted(tile, step) for step in STEPS]
    early, weights = lax.optimization_barrier((jnp.stack(around[:3]), weights))
    weights = in_vmem(weights)
    swapped_early = swapped(early, 0, 2)
    last, _ = lax.optimization_barrier((around[3], early))
    late = last[None]
    part0 = jnp.concatenate([early, late])
    part2 = jnp.concatenate([swapped_early, swapped(late, 0, 2)])
    lines = pltpu.VMEM((LENGTH, 128), f32)
    sums = pltpu.VMEM((2 * LENGTH, 128), f32)
    work = [(LENGTH, 128), (SIDE * RIGHT_LINE, 128), (LENGTH, 128), (SIDE * RIGHT_LINE, 128)]
    cost = 1 << 10
    outer, centred0, gate0, valid0 = call(
        first_kernel, "first", cost, (sums, lines, lines, lines), work, in_vmem(part0), in_vmem(own), weights
    )
    part2, outer = lax.optimization_barrier((part2, outer))
    part1 = swapped(part0, 0, 1)
    outer = call(next_kernel, "second", cost, sums, work, in_vmem(part1), weights, in_vmem(outer))
    part3 = swapped(part2, 0, 1)
    outer = call(next_kernel, "third", cost, sums, work, in_vmem(part2), weights, in_vmem(outer))
    part3, outer = lax.optimization_barrier((part3, outer))
    return call(
        last_kernel, "last", cost, jax.ShapeDtypeStruct(pair.shape, f32),
        work + [(2 * LENGTH, 128)] + 5 * [(LENGTH, 128)] + [(8 * ROWS, 128), (ROWS, 128), (ROWS, 128)],
        *map(in_vmem, (part0, part1, part2, part3, outer, centred0, gate0, valid0, own)),
        weights,
    )


def solution(mesh):
    def body(pair, *rest):
        compact = (
            mesh.shape["row"] == mesh.shape["col"] == SPLIT
            and pair.shape == (SIDE, SIDE, 128)
            and rest[1].shape == (128, 512)
        )
        return (compact_plan if compact else split_plan)(pair, *rest)

    return jax.shard_map(
        body,
        mesh=mesh,
        in_specs=(
            P(("grp", "row"), "col", None),
            P(("grp", "row"), "col"),
            P(),
            P(),
            P(),
            P(),
            P(),
            P(),
        ),
        out_specs=P(("grp", "row"), "col", None),
        check_vma=False,
    )
```

```python
import jax
import jax.numpy as jnp
from jax import lax
from jax.experimental import pallas as pl
from jax.experimental.pallas import tpu as pltpu
from jax.sharding import PartitionSpec as P

MASKED = 64.0
SPLIT = 4
SIDE = 10
MAIN = 8
REST = SIDE - MAIN
ROWS = 112
WIDTH = SIDE * SPLIT


def layer_norm(value):
    mean = jnp.mean(value, axis=-1, keepdims=True)
    centred = value - mean
    variance = jnp.mean(centred * centred, axis=-1, keepdims=True)
    return centred * lax.rsqrt(variance + 1e-05)


def project(pair, pair_mask, proj_weight, gate_weight):
    normed = layer_norm(pair)
    proj = jnp.einsum("ijc,cd->ijd", normed, proj_weight, precision=lax.Precision.HIGHEST)
    hidden = proj_weight.shape[1] // 4
    valid = pair_mask.astype(jnp.float32)[:, :, None]
    left = jax.nn.sigmoid(proj[..., :hidden]) * proj[..., hidden : 2 * hidden] * valid
    right = jax.nn.sigmoid(proj[..., 2 * hidden : 3 * hidden]) * proj[..., 3 * hidden :] * valid
    gate = jax.nn.sigmoid(
        jnp.einsum("ijc,cd->ijd", normed, gate_weight, precision=lax.Precision.HIGHEST)
    )
    left = jnp.transpose(left.astype(jnp.bfloat16), (2, 0, 1))
    right = jnp.transpose(right.astype(jnp.bfloat16), (2, 0, 1))
    return (left, right, gate)


def finish(pair, summed, gate, final_weight):
    normed = layer_norm(jnp.transpose(summed, (1, 2, 0)))
    return pair + gate * jnp.einsum(
        "ijh,hc->ijc", normed, final_weight, precision=lax.Precision.HIGHEST
    )


def split_plan(pair, pair_mask, out_proj, out_gate, out_final, in_proj, in_gate, in_final):
    left, right, gate = project(pair, pair_mask, out_proj, out_gate)
    outer_terms = jnp.einsum(
        "hik,hjk->hij",
        left,
        lax.all_gather(right, "row", axis=1, tiled=True),
        preferred_element_type=jnp.float32,
    )
    outer = lax.psum_scatter(
        outer_terms.astype(jnp.bfloat16), "col", scatter_dimension=2, tiled=True
    ).astype(jnp.float32)
    middle = finish(pair, outer, gate, out_final)
    left2, right2, gate2 = project(middle, pair_mask, in_proj, in_gate)
    inner_terms = jnp.einsum(
        "hki,hkj->hij",
        lax.all_gather(left2, "col", axis=2, tiled=True),
        right2,
        preferred_element_type=jnp.float32,
    )
    inner = lax.psum_scatter(
        inner_terms.astype(jnp.bfloat16), "row", scatter_dimension=1, tiled=True
    ).astype(jnp.float32)
    return finish(middle, inner, gate2, in_final)


def sigmoid(value):
    return 0.5 * jnp.tanh(0.5 * value) + 0.5


def dot(value, weight):
    return jnp.dot(value.astype(jnp.bfloat16), weight, preferred_element_type=jnp.float32)


def scaled(centred):
    return centred * lax.rsqrt(jnp.mean(centred * centred, axis=-1, keepdims=True) + 1e-05)


def rest_rows(k):
    return 80 + 16 * k


def pack_kernel(pair_ref, mask_ref, tile_ref, own_ref, valid_ref, pair_vmem, mask_vmem, sems):
    pair_copy = pltpu.make_async_copy(pair_ref, pair_vmem, sems.at[0])
    mask_copy = pltpu.make_async_copy(mask_ref, mask_vmem, sems.at[1])
    pair_copy.start()
    mask_copy.start()
    rest = pl.ds(MAIN * SIDE, ROWS - MAIN * SIDE)
    own_ref[rest, :] = jnp.zeros((ROWS - MAIN * SIDE, 128), own_ref.dtype)
    valid_ref[rest, :] = jnp.zeros((ROWS - MAIN * SIDE, 128), valid_ref.dtype)
    mask_copy.wait()
    valid = mask_vmem[...].astype(jnp.float32)
    for k in range(SIDE):
        column = jnp.broadcast_to(valid[:, k : k + 1], (SIDE, 128))
        valid_ref[pl.ds(MAIN * k, MAIN), :] = column[:MAIN]
        for e in range(REST):
            valid_ref[pl.ds(rest_rows(e) + k, 1), :] = column[MAIN + e : MAIN + e + 1]
    pair_copy.wait()
    for i in range(SIDE):
        at = pl.ds(i, SIDE, stride=MAIN) if i < MAIN else pl.ds(rest_rows(i - MAIN), SIDE)
        own_ref[at, :] = pair_vmem[i]
    own = own_ref[...]
    centred = own - jnp.mean(own, axis=-1, keepdims=True)
    tile_ref[...] = jnp.where(valid_ref[...] > 0.5, centred, MASKED).astype(tile_ref.dtype)


OUT_PROJ, OUT_GATE, OUT_FINAL, IN_PROJ, IN_GATE, IN_FINAL, WEIGHTS = 0, 512, 640, 768, 1280, 1408, 1536


def weights_kernel(*refs):
    start = 0
    for weight_ref in refs[:-1]:
        width = weight_ref.shape[1]
        refs[-1][:, pl.ds(start, width)] = weight_ref[...].astype(refs[-1].dtype)
        start += width


def to_lines(target, base, tile, slot, slots, line):
    for k in range(SIDE):
        target[pl.ds(base + line * k + MAIN * slot, MAIN), :] = tile[MAIN * k : MAIN * (k + 1)]
    for e in range(REST):
        target[pl.ds(base + MAIN * slots + REST * slot + e, SIDE, stride=line), :] = tile[
            rest_rows(e) : rest_rows(e) + SIDE
        ]


RIGHT_LINE = 24
LENGTH = SIDE * WIDTH
GROUP = 4


def add_terms(tiles, other, proj_weight, before_ref, outer_ref, lines_ref, right_lines_ref, left_ref, right_ref):
    for slot in range(SPLIT):
        to_lines(lines_ref, 0, tiles[slot].astype(jnp.float32), slot, SPLIT, WIDTH)
    to_lines(right_lines_ref, 0, tiles[0].astype(jnp.float32), 0, 2, RIGHT_LINE)
    to_lines(right_lines_ref, 0, tiles[other].astype(jnp.float32), 1, 2, RIGHT_LINE)
    raw = jnp.concatenate([lines_ref[...], right_lines_ref[...]], axis=0)
    normed = scaled(split_lines(raw)[0])
    proj = dot(normed[:LENGTH], proj_weight[:, :256])
    left_ref[...] = sigmoid(proj[:, :128]) * proj[:, 128:]
    proj = dot(normed[LENGTH:], proj_weight[:, 256:])
    right_ref[...] = sigmoid(proj[:, :128]) * proj[:, 128:]

    for g in range(2 * SIDE // GROUP):
        at = [pl.ds((g * GROUP + t) * WIDTH, WIDTH) for t in range(GROUP)]
        sums = [None if before_ref is None else before_ref[at[t], :] for t in range(GROUP)]
        for k in range(SIDE):
            rows = left_ref[pl.ds(k * WIDTH, WIDTH), :]
            for t in range(GROUP):
                one = right_ref[pl.ds(k * RIGHT_LINE + g * GROUP + t, 1), :]
                term = rows * jnp.broadcast_to(one, rows.shape)
                sums[t] = term if sums[t] is None else sums[t] + term
        for t in range(GROUP):
            outer_ref[at[t], :] = sums[t]


def split_lines(raw):
    valid = raw < 0.5 * MASKED
    return jnp.where(valid, raw, 0.0), valid


def other_slot():
    before = lax.rem(lax.axis_index("row") - lax.axis_index("col") + SPLIT, SPLIT)
    place = jnp.int32(0)
    for number, step in enumerate(STEPS):
        place = jnp.where(before == step, number + 1, place)
    return place


def other_part():
    return jnp.bitwise_xor(lax.axis_index("row"), lax.axis_index("col"))


def first_kernel(tiles, out_proj_ref, outer_ref, *scratch):
    add_terms(tiles, other_slot(), out_proj_ref[...].astype(jnp.bfloat16), None, outer_ref, *scratch)


def next_kernel(tiles, weights_ref, before_ref, outer_ref, *scratch):
    add_terms(tiles, other_slot(), weights_ref[:, pl.ds(OUT_PROJ, 512)], before_ref, outer_ref, *scratch)


def gate_kernel(tiles, own_tiles, own_ref, weights_ref, before_ref, outer_ref, centred_ref, gate_ref, valid_ref, *scratch):
    add_terms(tiles, other_slot(), weights_ref[:, pl.ds(OUT_PROJ, 512)], before_ref, outer_ref, *scratch[:-1])
    lines_ref = scratch[-1]
    for slot in range(SPLIT):
        to_lines(lines_ref, 0, own_tiles[slot].astype(jnp.float32), slot, SPLIT, WIDTH)
    centred, valid = split_lines(lines_ref[...])
    centred_ref[...] = centred
    valid_ref[...] = jnp.where(valid, 1.0, 0.0)
    own = own_ref[...]
    own = own - jnp.mean(own, axis=-1, keepdims=True)
    to_lines(centred_ref, 0, own, 0, SPLIT, WIDTH)
    gate_ref[...] = sigmoid(dot(scaled(centred_ref[...]), weights_ref[:, pl.ds(OUT_GATE, 128)]))


def last_kernel(
    part0, part1, part2, part3, before_ref, centred0_ref, gate0_ref, valid0_ref, own_ref,
    weights_ref,
    result_ref,
    lines_ref, right_lines_ref, left_ref, right_ref, outer_ref, block_ref, left2_ref, right2_ref, mid_ref, normed_ref,
    pieces_ref, flat_ref, flat2_ref,
):
    for number, tiles in enumerate((part0, part1, part2, part3)):
        @pl.when(other_part() == number)
        def _():
            for slot in range(SPLIT):
                to_lines(block_ref, 0, tiles[slot].astype(jnp.float32), slot, SPLIT, WIDTH)

    add_terms(
        part3, other_slot(), weights_ref[:, pl.ds(OUT_PROJ, 512)], before_ref, outer_ref,
        lines_ref, right_lines_ref, left_ref, right_ref,
    )

    def sums_of(slot):
        return [
            outer_ref[pl.ds(slot * MAIN * WIDTH, MAIN * WIDTH), :],
            outer_ref[pl.ds((2 * MAIN + REST * slot) * WIDTH, REST * WIDTH), :],
        ]

    centred1, valid1 = split_lines(block_ref[...])
    gate1 = sigmoid(dot(scaled(centred1), weights_ref[:, pl.ds(OUT_GATE, 128)]))
    gate = jnp.concatenate([gate0_ref[...], gate1], axis=0)
    centred = jnp.concatenate([centred0_ref[...], centred1], axis=0)
    change = gate * dot(layer_norm(jnp.concatenate(sums_of(1) + sums_of(0), axis=0)), weights_ref[:, pl.ds(OUT_FINAL, 128)])
    normed = layer_norm(centred + change)
    mid_ref[...] = change[:LENGTH]
    normed_ref[...] = normed[:LENGTH]
    proj = dot(normed[:LENGTH], weights_ref[:, pl.ds(IN_PROJ + 256, 256)])
    right2_ref[...] = jnp.where(valid0_ref[...] > 0.5, sigmoid(proj[:, :128]) * proj[:, 128:], 0.0)
    proj = dot(normed[LENGTH:], weights_ref[:, pl.ds(IN_PROJ, 256)])
    left2_ref[...] = jnp.where(valid1, sigmoid(proj[:, :128]) * proj[:, 128:], 0.0)

    for j in range(SIDE):
        right = right2_ref[pl.ds(j * WIDTH, WIDTH), :]
        for i in range(SIDE):
            product = left2_ref[pl.ds(i * WIDTH, WIDTH), :] * right
            folded = product[:8]
            for t in range(1, WIDTH // 8):
                folded = folded + product[8 * t : 8 * (t + 1)]
            at = MAIN * j + i if i < MAIN else rest_rows(i - MAIN) + j
            pieces_ref[pl.ds(8 * at, 8), :] = folded
    inner = pieces_ref[pl.ds(0, ROWS, stride=8), :]
    for t in range(1, 8):
        inner = inner + pieces_ref[pl.ds(t, ROWS, stride=8), :]

    def own_rows(source_ref, flat_ref):
        for k in range(SIDE):
            flat_ref[pl.ds(MAIN * k, MAIN), :] = source_ref[pl.ds(WIDTH * k, MAIN), :]
        for e in range(REST):
            flat_ref[pl.ds(rest_rows(e), SIDE), :] = source_ref[pl.ds(MAIN * SPLIT + e, SIDE, stride=WIDTH), :]
        return flat_ref[...]

    mid = own_ref[...] + own_rows(mid_ref, flat_ref)
    gate = sigmoid(dot(own_rows(normed_ref, flat2_ref), weights_ref[:, pl.ds(IN_GATE, 128)]))
    result = mid + gate * dot(layer_norm(inner), weights_ref[:, pl.ds(IN_FINAL, 128)])
    for k in range(SIDE):
        result_ref[pl.ds(0, MAIN), k, :] = result[MAIN * k : MAIN * (k + 1)]
        for e in range(REST):
            result_ref[MAIN + e, pl.ds(k, 1), :] = result[rest_rows(e) + k : rest_rows(e) + k + 1]


def swapped(value, rows, cols):
    pairs = [
        (r * SPLIT + c, (r ^ rows) * SPLIT + (c ^ cols)) for r in range(SPLIT) for c in range(SPLIT)
    ]
    return lax.ppermute(value, ("row", "col"), pairs)


STEPS = (1, 2, 3)


def shifted(value, step, cols=0):
    pairs = [
        (r * SPLIT + c, (r + step) % SPLIT * SPLIT + (c ^ cols)) for r in range(SPLIT) for c in range(SPLIT)
    ]
    return lax.ppermute(value, ("row", "col"), pairs)


def in_vmem(value):
    return pltpu.with_memory_space_constraint(value, pltpu.VMEM)


def call(kernel, name, cycles, out, scratch, *operands, grant=32 << 20, **more):
    return pl.pallas_call(
        kernel,
        out_shape=out,
        scratch_shapes=[pltpu.VMEM(one, jnp.float32) if isinstance(one, tuple) else one for one in scratch],
        cost_estimate=pl.CostEstimate(flops=cycles, bytes_accessed=0, transcendentals=0),
        compiler_params=pltpu.CompilerParams(vmem_limit_bytes=grant),
        name=name,
        **more,
    )(*operands)


def compact_plan(pair, pair_mask, *weights):
    f32 = jnp.float32
    tile, own = call(
        pack_kernel, "pack", 1000, (pltpu.VMEM((ROWS, 128), jnp.bfloat16), pltpu.VMEM((ROWS, 128), f32)),
        [(ROWS, 128), pair.shape, pltpu.VMEM(pair_mask.shape, jnp.int32), pltpu.SemaphoreType.DMA((2,))],
        pair, pair_mask, grant=None, in_specs=2 * [pl.BlockSpec(memory_space=pl.ANY)],
    )
    around = [tile] + [shifted(tile, step) for step in STEPS]
    aslant = shifted(tile, STEPS[2], 2)
    early = jnp.stack(around[:3])
    swapped_early = swapped(early, 0, 2)
    late, _ = lax.optimization_barrier((around[3], early))
    part0 = jnp.concatenate([early, late[None]])
    lines = pltpu.VMEM((LENGTH, 128), f32)
    sums = pltpu.VMEM((2 * LENGTH, 128), f32)
    work = [(LENGTH, 128), (SIDE * RIGHT_LINE, 128), (LENGTH, 128), (SIDE * RIGHT_LINE, 128)]
    cost = 1 << 10
    outer = call(first_kernel, "first", cost, sums, work, in_vmem(part0), in_vmem(weights[0]))
    outer, *weights = lax.optimization_barrier((outer, *weights))
    weights = call(
        weights_kernel, "weights", 1000, pltpu.VMEM((128, WEIGHTS), jnp.bfloat16), [], *weights, grant=None
    )
    aslant, swapped_early, outer, weights = lax.optimization_barrier((aslant, swapped_early, outer, weights))
    part2 = jnp.concatenate([swapped_early, aslant[None]])
    weights = in_vmem(weights)
    part1 = swapped(part0, 0, 1)
    outer, centred0, gate0, valid0 = call(
        gate_kernel, "second", cost, (sums, lines, lines, lines), work + [(LENGTH, 128)],
        *map(in_vmem, (part1, part0, own)), weights, in_vmem(outer),
    )
    part3 = swapped(part2, 0, 1)
    outer = call(next_kernel, "third", cost, sums, work, in_vmem(part2), weights, in_vmem(outer))
    part3, outer = lax.optimization_barrier((part3, outer))
    return call(
        last_kernel, "last", cost, jax.ShapeDtypeStruct(pair.shape, f32),
        work + [(2 * LENGTH, 128)] + 5 * [(LENGTH, 128)] + [(8 * ROWS, 128), (ROWS, 128), (ROWS, 128)],
        *map(in_vmem, (part0, part1, part2, part3, outer, centred0, gate0, valid0, own)),
        weights,
    )


def solution(mesh):
    def body(pair, *rest):
        compact = (
            mesh.shape["row"] == mesh.shape["col"] == SPLIT
            and pair.shape == (SIDE, SIDE, 128)
            and rest[1].shape == (128, 512)
        )
        return (compact_plan if compact else split_plan)(pair, *rest)

    return jax.shard_map(
        body,
        mesh=mesh,
        in_specs=(
            P(("grp", "row"), "col", None),
            P(("grp", "row"), "col"),
            P(),
            P(),
            P(),
            P(),
            P(),
            P(),
        ),
        out_specs=P(("grp", "row"), "col", None),
        check_vma=False,
    )
```

```python
import jax
import jax.numpy as jnp
from jax import lax
from jax.experimental import pallas as pl
from jax.experimental.pallas import tpu as pltpu
from jax.sharding import PartitionSpec as P

MASKED = 64.0
SPLIT = 4
SIDE = 10
MAIN = 8
REST = SIDE - MAIN
ROWS = 112
WIDTH = SIDE * SPLIT


def layer_norm(value):
    mean = jnp.mean(value, axis=-1, keepdims=True)
    centred = value - mean
    variance = jnp.mean(centred * centred, axis=-1, keepdims=True)
    return centred * lax.rsqrt(variance + 1e-05)


def project(pair, pair_mask, proj_weight, gate_weight):
    normed = layer_norm(pair)
    proj = jnp.einsum("ijc,cd->ijd", normed, proj_weight, precision=lax.Precision.HIGHEST)
    hidden = proj_weight.shape[1] // 4
    valid = pair_mask.astype(jnp.float32)[:, :, None]
    left = jax.nn.sigmoid(proj[..., :hidden]) * proj[..., hidden : 2 * hidden] * valid
    right = jax.nn.sigmoid(proj[..., 2 * hidden : 3 * hidden]) * proj[..., 3 * hidden :] * valid
    gate = jax.nn.sigmoid(
        jnp.einsum("ijc,cd->ijd", normed, gate_weight, precision=lax.Precision.HIGHEST)
    )
    left = jnp.transpose(left.astype(jnp.bfloat16), (2, 0, 1))
    right = jnp.transpose(right.astype(jnp.bfloat16), (2, 0, 1))
    return (left, right, gate)


def finish(pair, summed, gate, final_weight):
    normed = layer_norm(jnp.transpose(summed, (1, 2, 0)))
    return pair + gate * jnp.einsum(
        "ijh,hc->ijc", normed, final_weight, precision=lax.Precision.HIGHEST
    )


def split_plan(pair, pair_mask, out_proj, out_gate, out_final, in_proj, in_gate, in_final):
    left, right, gate = project(pair, pair_mask, out_proj, out_gate)
    outer_terms = jnp.einsum(
        "hik,hjk->hij",
        left,
        lax.all_gather(right, "row", axis=1, tiled=True),
        preferred_element_type=jnp.float32,
    )
    outer = lax.psum_scatter(
        outer_terms.astype(jnp.bfloat16), "col", scatter_dimension=2, tiled=True
    ).astype(jnp.float32)
    middle = finish(pair, outer, gate, out_final)
    left2, right2, gate2 = project(middle, pair_mask, in_proj, in_gate)
    inner_terms = jnp.einsum(
        "hki,hkj->hij",
        lax.all_gather(left2, "col", axis=2, tiled=True),
        right2,
        preferred_element_type=jnp.float32,
    )
    inner = lax.psum_scatter(
        inner_terms.astype(jnp.bfloat16), "row", scatter_dimension=1, tiled=True
    ).astype(jnp.float32)
    return finish(middle, inner, gate2, in_final)


def gated(half_gate, half_value):
    return (jnp.tanh(half_gate) + 1.0) * half_value


def halved(weight):
    return (0.5 * weight).astype(jnp.bfloat16)


def dot(value, weight):
    return jnp.dot(value.astype(jnp.bfloat16), weight, preferred_element_type=jnp.float32)


def layer_norm_once(value):
    mean = jnp.mean(value, axis=-1, keepdims=True)
    variance = jnp.maximum(jnp.mean(value * value, axis=-1, keepdims=True) - mean * mean, 0.0)
    return (value - mean) * lax.rsqrt(variance + 1e-05)


def scaled(centred):
    return centred * lax.rsqrt(jnp.mean(centred * centred, axis=-1, keepdims=True) + 1e-05)


def rest_rows(k):
    return 80 + 16 * k


def pack_kernel(pair_ref, mask_ref, tile_ref, own_ref, valid_ref, pair_vmem, mask_vmem, sems):
    pair_copy = pltpu.make_async_copy(pair_ref, pair_vmem, sems.at[0])
    mask_copy = pltpu.make_async_copy(mask_ref, mask_vmem, sems.at[1])
    pair_copy.start()
    mask_copy.start()
    rest = pl.ds(MAIN * SIDE, ROWS - MAIN * SIDE)
    own_ref[rest, :] = jnp.zeros((ROWS - MAIN * SIDE, 128), own_ref.dtype)
    valid_ref[rest, :] = jnp.zeros((ROWS - MAIN * SIDE, 128), valid_ref.dtype)
    mask_copy.wait()
    valid = mask_vmem[...].astype(jnp.float32)
    for k in range(SIDE):
        column = jnp.broadcast_to(valid[:, k : k + 1], (SIDE, 128))
        valid_ref[pl.ds(MAIN * k, MAIN), :] = column[:MAIN]
        for e in range(REST):
            valid_ref[pl.ds(rest_rows(e) + k, 1), :] = column[MAIN + e : MAIN + e + 1]
    pair_copy.wait()
    for i in range(SIDE):
        at = pl.ds(i, SIDE, stride=MAIN) if i < MAIN else pl.ds(rest_rows(i - MAIN), SIDE)
        own_ref[at, :] = pair_vmem[i]
    own = own_ref[...]
    centred = own - jnp.mean(own, axis=-1, keepdims=True)
    tile_ref[...] = jnp.where(valid_ref[...] > 0.5, centred, MASKED).astype(tile_ref.dtype)


OUT_PROJ, OUT_GATE, OUT_FINAL, IN_PROJ, IN_GATE, IN_FINAL, WEIGHTS = 0, 512, 640, 768, 1280, 1408, 1536


def weights_kernel(*refs):
    start = 0
    for weight_ref in refs[:-1]:
        width = weight_ref.shape[1]
        refs[-1][:, pl.ds(start, width)] = halved(weight_ref[...])
        start += width


def to_lines(target, base, tile, slot, slots, line):
    for k in range(SIDE):
        target[pl.ds(base + line * k + MAIN * slot, MAIN), :] = tile[MAIN * k : MAIN * (k + 1)]
    for e in range(REST):
        target[pl.ds(base + MAIN * slots + REST * slot + e, SIDE, stride=line), :] = tile[
            rest_rows(e) : rest_rows(e) + SIDE
        ]


RIGHT_LINE = 24
LENGTH = SIDE * WIDTH
GROUP = 4


def add_terms(tiles, other, proj_weight, before_ref, outer_ref, lines_ref, right_lines_ref, left_ref, right_ref):
    for slot in range(SPLIT):
        to_lines(lines_ref, 0, tiles[slot].astype(jnp.float32), slot, SPLIT, WIDTH)
    to_lines(right_lines_ref, 0, tiles[0].astype(jnp.float32), 0, 2, RIGHT_LINE)
    to_lines(right_lines_ref, 0, tiles[other].astype(jnp.float32), 1, 2, RIGHT_LINE)
    raw = jnp.concatenate([lines_ref[...], right_lines_ref[...]], axis=0)
    normed = scaled(split_lines(raw)[0])
    proj = dot(normed[:LENGTH], proj_weight[:, :256])
    left_ref[...] = gated(proj[:, :128], proj[:, 128:])
    proj = dot(normed[LENGTH:], proj_weight[:, 256:])
    right_ref[...] = gated(proj[:, :128], proj[:, 128:])

    for g in range(2 * SIDE // GROUP):
        at = [pl.ds((g * GROUP + t) * WIDTH, WIDTH) for t in range(GROUP)]
        sums = [None if before_ref is None else before_ref[at[t], :] for t in range(GROUP)]
        for k in range(SIDE):
            rows = left_ref[pl.ds(k * WIDTH, WIDTH), :]
            for t in range(GROUP):
                one = right_ref[pl.ds(k * RIGHT_LINE + g * GROUP + t, 1), :]
                term = rows * jnp.broadcast_to(one, rows.shape)
                sums[t] = term if sums[t] is None else sums[t] + term
        for t in range(GROUP):
            outer_ref[at[t], :] = sums[t]


def split_lines(raw):
    valid = raw < 0.5 * MASKED
    return jnp.where(valid, raw, 0.0), valid


def other_slot():
    before = lax.rem(lax.axis_index("row") - lax.axis_index("col") + SPLIT, SPLIT)
    place = jnp.int32(0)
    for number, step in enumerate(STEPS):
        place = jnp.where(before == step, number + 1, place)
    return place


def other_part():
    return jnp.bitwise_xor(lax.axis_index("row"), lax.axis_index("col"))


def first_kernel(tiles, out_proj_ref, outer_ref, *scratch):
    add_terms(tiles, other_slot(), halved(out_proj_ref[...]), None, outer_ref, *scratch)


def next_kernel(tiles, weights_ref, before_ref, outer_ref, *scratch):
    add_terms(tiles, other_slot(), weights_ref[:, pl.ds(OUT_PROJ, 512)], before_ref, outer_ref, *scratch)


def gate_kernel(tiles, own_tiles, own_ref, weights_ref, before_ref, outer_ref, centred_ref, half_gate_ref, valid_ref, *scratch):
    add_terms(tiles, other_slot(), weights_ref[:, pl.ds(OUT_PROJ, 512)], before_ref, outer_ref, *scratch[:-1])
    lines_ref = scratch[-1]
    for slot in range(SPLIT):
        to_lines(lines_ref, 0, own_tiles[slot].astype(jnp.float32), slot, SPLIT, WIDTH)
    centred, valid = split_lines(lines_ref[...])
    centred_ref[...] = centred
    valid_ref[...] = jnp.where(valid, 1.0, 0.0)
    own = own_ref[...]
    own = own - jnp.mean(own, axis=-1, keepdims=True)
    to_lines(centred_ref, 0, own, 0, SPLIT, WIDTH)
    half_gate_ref[...] = dot(scaled(centred_ref[...]), weights_ref[:, pl.ds(OUT_GATE, 128)])


def last_kernel(
    part0, part1, part2, part3, before_ref, centred0_ref, half_gate0_ref, valid0_ref, own_ref,
    weights_ref,
    result_ref,
    lines_ref, right_lines_ref, left_ref, right_ref, outer_ref, block_ref, left2_ref, right2_ref, mid_ref, normed_ref,
    pieces_ref, flat_ref, flat2_ref,
):
    for number, tiles in enumerate((part0, part1, part2, part3)):
        @pl.when(other_part() == number)
        def _():
            for slot in range(SPLIT):
                to_lines(block_ref, 0, tiles[slot].astype(jnp.float32), slot, SPLIT, WIDTH)

    add_terms(
        part3, other_slot(), weights_ref[:, pl.ds(OUT_PROJ, 512)], before_ref, outer_ref,
        lines_ref, right_lines_ref, left_ref, right_ref,
    )

    def sums_of(slot):
        return [
            outer_ref[pl.ds(slot * MAIN * WIDTH, MAIN * WIDTH), :],
            outer_ref[pl.ds((2 * MAIN + REST * slot) * WIDTH, REST * WIDTH), :],
        ]

    centred1, valid1 = split_lines(block_ref[...])
    half_gate1 = dot(scaled(centred1), weights_ref[:, pl.ds(OUT_GATE, 128)])
    half_gate = jnp.concatenate([half_gate0_ref[...], half_gate1], axis=0)
    centred = jnp.concatenate([centred0_ref[...], centred1], axis=0)
    normed = layer_norm(jnp.concatenate(sums_of(1) + sums_of(0), axis=0))
    change = gated(half_gate, dot(normed, weights_ref[:, pl.ds(OUT_FINAL, 128)]))
    normed = layer_norm(centred + change)
    mid_ref[...] = change[:LENGTH]
    normed_ref[...] = normed[:LENGTH]
    proj = dot(normed[:LENGTH], weights_ref[:, pl.ds(IN_PROJ + 256, 256)])
    right2_ref[...] = valid0_ref[...] * gated(proj[:, :128], proj[:, 128:])
    proj = dot(normed[LENGTH:], weights_ref[:, pl.ds(IN_PROJ, 256)])
    left2_ref[...] = jnp.where(valid1, gated(proj[:, :128], proj[:, 128:]), 0.0)

    for j in range(SIDE):
        right = right2_ref[pl.ds(j * WIDTH, WIDTH), :]
        for i in range(SIDE):
            product = left2_ref[pl.ds(i * WIDTH, WIDTH), :] * right
            folded = product[:8]
            for t in range(1, WIDTH // 8):
                folded = folded + product[8 * t : 8 * (t + 1)]
            at = MAIN * j + i if i < MAIN else rest_rows(i - MAIN) + j
            pieces_ref[pl.ds(8 * at, 8), :] = folded
    inner = pieces_ref[pl.ds(0, ROWS, stride=8), :]
    for t in range(1, 8):
        inner = inner + pieces_ref[pl.ds(t, ROWS, stride=8), :]

    def own_rows(source_ref, flat_ref):
        for k in range(SIDE):
            flat_ref[pl.ds(MAIN * k, MAIN), :] = source_ref[pl.ds(WIDTH * k, MAIN), :]
        for e in range(REST):
            flat_ref[pl.ds(rest_rows(e), SIDE), :] = source_ref[pl.ds(MAIN * SPLIT + e, SIDE, stride=WIDTH), :]
        return flat_ref[...]

    mid = own_ref[...] + own_rows(mid_ref, flat_ref)
    half_gate = dot(own_rows(normed_ref, flat2_ref), weights_ref[:, pl.ds(IN_GATE, 128)])
    result = mid + gated(half_gate, dot(layer_norm_once(inner), weights_ref[:, pl.ds(IN_FINAL, 128)]))
    for k in range(SIDE):
        result_ref[pl.ds(0, MAIN), k, :] = result[MAIN * k : MAIN * (k + 1)]
        for e in range(REST):
            result_ref[MAIN + e, pl.ds(k, 1), :] = result[rest_rows(e) + k : rest_rows(e) + k + 1]


def swapped(value, rows, cols):
    pairs = [
        (r * SPLIT + c, (r ^ rows) * SPLIT + (c ^ cols)) for r in range(SPLIT) for c in range(SPLIT)
    ]
    return lax.ppermute(value, ("row", "col"), pairs)


STEPS = (1, 2, 3)


def shifted(value, step, cols=0):
    pairs = [
        (r * SPLIT + c, (r + step) % SPLIT * SPLIT + (c ^ cols)) for r in range(SPLIT) for c in range(SPLIT)
    ]
    return lax.ppermute(value, ("row", "col"), pairs)


def in_vmem(value):
    return pltpu.with_memory_space_constraint(value, pltpu.VMEM)


def call(kernel, name, cycles, out, scratch, *operands, grant=32 << 20, **more):
    return pl.pallas_call(
        kernel,
        out_shape=out,
        scratch_shapes=[pltpu.VMEM(one, jnp.float32) if isinstance(one, tuple) else one for one in scratch],
        cost_estimate=pl.CostEstimate(flops=cycles, bytes_accessed=0, transcendentals=0),
        compiler_params=pltpu.CompilerParams(vmem_limit_bytes=grant),
        name=name,
        **more,
    )(*operands)


def compact_plan(pair, pair_mask, *weights):
    f32 = jnp.float32
    tile, own = call(
        pack_kernel, "pack", 1000, (pltpu.VMEM((ROWS, 128), jnp.bfloat16), pltpu.VMEM((ROWS, 128), f32)),
        [(ROWS, 128), pair.shape, pltpu.VMEM(pair_mask.shape, jnp.int32), pltpu.SemaphoreType.DMA((2,))],
        pair, pair_mask, grant=None, in_specs=2 * [pl.BlockSpec(memory_space=pl.ANY)],
    )
    around = [tile] + [shifted(tile, step) for step in STEPS]
    aslant = shifted(tile, STEPS[2], 2)
    early = jnp.stack(around[:3])
    swapped_early = swapped(early, 0, 2)
    late, _ = lax.optimization_barrier((around[3], early))
    part0 = jnp.concatenate([early, late[None]])
    lines = pltpu.VMEM((LENGTH, 128), f32)
    sums = pltpu.VMEM((2 * LENGTH, 128), f32)
    work = [(LENGTH, 128), (SIDE * RIGHT_LINE, 128), (LENGTH, 128), (SIDE * RIGHT_LINE, 128)]
    cost = 1 << 10
    outer = call(first_kernel, "first", cost, sums, work, in_vmem(part0), in_vmem(weights[0]))
    outer, *weights = lax.optimization_barrier((outer, *weights))
    weights = call(
        weights_kernel, "weights", 1000, pltpu.VMEM((128, WEIGHTS), jnp.bfloat16), [], *weights, grant=None
    )
    aslant, swapped_early, outer, weights = lax.optimization_barrier((aslant, swapped_early, outer, weights))
    part2 = jnp.concatenate([swapped_early, aslant[None]])
    weights = in_vmem(weights)
    part1 = swapped(part0, 0, 1)
    outer, centred0, gate0, valid0 = call(
        gate_kernel, "second", cost, (sums, lines, lines, lines), work + [(LENGTH, 128)],
        *map(in_vmem, (part1, part0, own)), weights, in_vmem(outer),
    )
    part3 = swapped(part2, 0, 1)
    outer = call(next_kernel, "third", cost, sums, work, in_vmem(part2), weights, in_vmem(outer))
    part3, outer = lax.optimization_barrier((part3, outer))
    return call(
        last_kernel, "last", cost, jax.ShapeDtypeStruct(pair.shape, f32),
        work + [(2 * LENGTH, 128)] + 5 * [(LENGTH, 128)] + [(8 * ROWS, 128), (ROWS, 128), (ROWS, 128)],
        *map(in_vmem, (part0, part1, part2, part3, outer, centred0, gate0, valid0, own)),
        weights,
    )


def solution(mesh):
    def body(pair, *rest):
        compact = (
            mesh.shape["row"] == mesh.shape["col"] == SPLIT
            and pair.shape == (SIDE, SIDE, 128)
            and rest[1].shape == (128, 512)
        )
        return (compact_plan if compact else split_plan)(pair, *rest)

    return jax.shard_map(
        body,
        mesh=mesh,
        in_specs=(
            P(("grp", "row"), "col", None),
            P(("grp", "row"), "col"),
            P(),
            P(),
            P(),
            P(),
            P(),
            P(),
        ),
        out_specs=P(("grp", "row"), "col", None),
        check_vma=False,
    )
```

```python
import jax
import jax.numpy as jnp
from jax import lax
from jax.experimental import pallas as pl
from jax.experimental.pallas import tpu as pltpu
from jax.sharding import PartitionSpec as P

MASKED = 64.0
SPLIT = 4
SIDE = 10
MAIN = 8
REST = SIDE - MAIN
ROWS = 112
WIDTH = SIDE * SPLIT


def layer_norm(value):
    mean = jnp.mean(value, axis=-1, keepdims=True)
    centred = value - mean
    variance = jnp.mean(centred * centred, axis=-1, keepdims=True)
    return centred * lax.rsqrt(variance + 1e-05)


def project(pair, pair_mask, proj_weight, gate_weight):
    normed = layer_norm(pair)
    proj = jnp.einsum("ijc,cd->ijd", normed, proj_weight, precision=lax.Precision.HIGHEST)
    hidden = proj_weight.shape[1] // 4
    valid = pair_mask.astype(jnp.float32)[:, :, None]
    left = jax.nn.sigmoid(proj[..., :hidden]) * proj[..., hidden : 2 * hidden] * valid
    right = jax.nn.sigmoid(proj[..., 2 * hidden : 3 * hidden]) * proj[..., 3 * hidden :] * valid
    gate = jax.nn.sigmoid(
        jnp.einsum("ijc,cd->ijd", normed, gate_weight, precision=lax.Precision.HIGHEST)
    )
    left = jnp.transpose(left.astype(jnp.bfloat16), (2, 0, 1))
    right = jnp.transpose(right.astype(jnp.bfloat16), (2, 0, 1))
    return (left, right, gate)


def finish(pair, summed, gate, final_weight):
    normed = layer_norm(jnp.transpose(summed, (1, 2, 0)))
    return pair + gate * jnp.einsum(
        "ijh,hc->ijc", normed, final_weight, precision=lax.Precision.HIGHEST
    )


def split_plan(pair, pair_mask, out_proj, out_gate, out_final, in_proj, in_gate, in_final):
    left, right, gate = project(pair, pair_mask, out_proj, out_gate)
    outer_terms = jnp.einsum(
        "hik,hjk->hij",
        left,
        lax.all_gather(right, "row", axis=1, tiled=True),
        preferred_element_type=jnp.float32,
    )
    outer = lax.psum_scatter(
        outer_terms.astype(jnp.bfloat16), "col", scatter_dimension=2, tiled=True
    ).astype(jnp.float32)
    middle = finish(pair, outer, gate, out_final)
    left2, right2, gate2 = project(middle, pair_mask, in_proj, in_gate)
    inner_terms = jnp.einsum(
        "hki,hkj->hij",
        lax.all_gather(left2, "col", axis=2, tiled=True),
        right2,
        preferred_element_type=jnp.float32,
    )
    inner = lax.psum_scatter(
        inner_terms.astype(jnp.bfloat16), "row", scatter_dimension=1, tiled=True
    ).astype(jnp.float32)
    return finish(middle, inner, gate2, in_final)


def gated(half_gate, half_value):
    return (jnp.tanh(half_gate) + 1.0) * half_value


def halved(weight):
    half = 0.5 * weight
    high = half.astype(jnp.bfloat16)
    low = (half - high.astype(jnp.float32)).astype(jnp.bfloat16)
    return jnp.concatenate([high, low], axis=0)


def dot(value, terms):
    value = value.astype(jnp.bfloat16)
    return jnp.dot(jnp.concatenate([value, value], axis=1), terms, preferred_element_type=jnp.float32)


def centre(value):
    return value - jnp.mean(value, axis=-1, keepdims=True)


def scale_of(centred):
    return lax.rsqrt(jnp.mean(centred * centred, axis=-1, keepdims=True) + 1e-05)


def rest_rows(k):
    return 80 + 16 * k


def pack_kernel(pair_ref, mask_ref, tile_ref, own_ref, valid_ref, pair_vmem, mask_vmem, sems):
    pair_copy = pltpu.make_async_copy(pair_ref, pair_vmem, sems.at[0])
    mask_copy = pltpu.make_async_copy(mask_ref, mask_vmem, sems.at[1])
    pair_copy.start()
    mask_copy.start()
    rest = pl.ds(MAIN * SIDE, ROWS - MAIN * SIDE)
    own_ref[rest, :] = jnp.zeros((ROWS - MAIN * SIDE, 128), own_ref.dtype)
    valid_ref[rest, :] = jnp.zeros((ROWS - MAIN * SIDE, 128), valid_ref.dtype)
    mask_copy.wait()
    valid = mask_vmem[...].astype(jnp.float32)
    for k in range(SIDE):
        column = jnp.broadcast_to(valid[:, k : k + 1], (SIDE, 128))
        valid_ref[pl.ds(MAIN * k, MAIN), :] = column[:MAIN]
        for e in range(REST):
            valid_ref[pl.ds(rest_rows(e) + k, 1), :] = column[MAIN + e : MAIN + e + 1]
    pair_copy.wait()
    for i in range(SIDE):
        at = pl.ds(i, SIDE, stride=MAIN) if i < MAIN else pl.ds(rest_rows(i - MAIN), SIDE)
        own_ref[at, :] = pair_vmem[i]
    own = own_ref[...]
    centred = own - jnp.mean(own, axis=-1, keepdims=True)
    tile_ref[...] = jnp.where(valid_ref[...] > 0.5, centred, MASKED).astype(tile_ref.dtype)


OUT_PROJ, OUT_GATE, OUT_FINAL, IN_PROJ, IN_GATE, IN_FINAL, WEIGHTS = 0, 512, 640, 768, 1280, 1408, 1536


def weights_kernel(*refs):
    start = 0
    for weight_ref in refs[:-1]:
        width = weight_ref.shape[1]
        refs[-1][:, pl.ds(start, width)] = halved(weight_ref[...])
        start += width


def to_lines(target, base, tile, slot, slots, line):
    for k in range(SIDE):
        target[pl.ds(base + line * k + MAIN * slot, MAIN), :] = tile[MAIN * k : MAIN * (k + 1)]
    for e in range(REST):
        target[pl.ds(base + MAIN * slots + REST * slot + e, SIDE, stride=line), :] = tile[
            rest_rows(e) : rest_rows(e) + SIDE
        ]


RIGHT_LINE = 24
LENGTH = SIDE * WIDTH
GROUP = 4


def add_terms(tiles, other, proj_weight, before_ref, outer_ref, lines_ref, right_lines_ref, left_ref, right_ref):
    for slot in range(SPLIT):
        to_lines(lines_ref, 0, tiles[slot].astype(jnp.float32), slot, SPLIT, WIDTH)
    to_lines(right_lines_ref, 0, tiles[0].astype(jnp.float32), 0, 2, RIGHT_LINE)
    to_lines(right_lines_ref, 0, tiles[other].astype(jnp.float32), 1, 2, RIGHT_LINE)
    raw = jnp.concatenate([lines_ref[...], right_lines_ref[...]], axis=0)
    centred = split_lines(raw)[0]
    scale = scale_of(centred)
    proj = dot(centred[:LENGTH], proj_weight[:, :256]) * scale[:LENGTH]
    left_ref[...] = gated(proj[:, :128], proj[:, 128:])
    proj = dot(centred[LENGTH:], proj_weight[:, 256:]) * scale[LENGTH:]
    right_ref[...] = gated(proj[:, :128], proj[:, 128:])

    for g in range(2 * SIDE // GROUP):
        at = [pl.ds((g * GROUP + t) * WIDTH, WIDTH) for t in range(GROUP)]
        sums = [None if before_ref is None else before_ref[at[t], :] for t in range(GROUP)]
        for k in range(SIDE):
            rows = left_ref[pl.ds(k * WIDTH, WIDTH), :]
            for t in range(GROUP):
                one = right_ref[pl.ds(k * RIGHT_LINE + g * GROUP + t, 1), :]
                term = rows * jnp.broadcast_to(one, rows.shape)
                sums[t] = term if sums[t] is None else sums[t] + term
        for t in range(GROUP):
            outer_ref[at[t], :] = sums[t]


def split_lines(raw):
    valid = raw < 0.5 * MASKED
    return jnp.where(valid, raw, 0.0), valid


def other_slot():
    before = lax.rem(lax.axis_index("row") - lax.axis_index("col") + SPLIT, SPLIT)
    place = jnp.int32(0)
    for number, step in enumerate(STEPS):
        place = jnp.where(before == step, number + 1, place)
    return place


def other_part():
    return jnp.bitwise_xor(lax.axis_index("row"), lax.axis_index("col"))


def first_kernel(tiles, out_proj_ref, outer_ref, *scratch):
    add_terms(tiles, other_slot(), halved(out_proj_ref[...]), None, outer_ref, *scratch)


def next_kernel(tiles, weights_ref, before_ref, outer_ref, *scratch):
    add_terms(tiles, other_slot(), weights_ref[:, pl.ds(OUT_PROJ, 512)], before_ref, outer_ref, *scratch)


def gate_kernel(tiles, own_tiles, own_ref, weights_ref, before_ref, outer_ref, centred_ref, half_gate_ref, valid_ref, *scratch):
    add_terms(tiles, other_slot(), weights_ref[:, pl.ds(OUT_PROJ, 512)], before_ref, outer_ref, *scratch[:-1])
    lines_ref = scratch[-1]
    for slot in range(SPLIT):
        to_lines(lines_ref, 0, own_tiles[slot].astype(jnp.float32), slot, SPLIT, WIDTH)
    centred, valid = split_lines(lines_ref[...])
    centred_ref[...] = centred
    valid_ref[...] = jnp.where(valid, 1.0, 0.0)
    own = own_ref[...]
    own = own - jnp.mean(own, axis=-1, keepdims=True)
    to_lines(centred_ref, 0, own, 0, SPLIT, WIDTH)
    centred = centred_ref[...]
    half_gate_ref[...] = dot(centred, weights_ref[:, pl.ds(OUT_GATE, 128)]) * scale_of(centred)


def last_kernel(
    part0, part1, part2, part3, before_ref, centred0_ref, half_gate0_ref, valid0_ref, own_ref,
    weights_ref,
    result_ref,
    lines_ref, right_lines_ref, left_ref, right_ref, outer_ref, block_ref, left2_ref, right2_ref, change_ref, normed_ref,
    pieces_ref, flat_ref, flat2_ref,
):
    for number, tiles in enumerate((part0, part1, part2, part3)):
        @pl.when(other_part() == number)
        def _():
            for slot in range(SPLIT):
                to_lines(block_ref, 0, tiles[slot].astype(jnp.float32), slot, SPLIT, WIDTH)

    add_terms(
        part3, other_slot(), weights_ref[:, pl.ds(OUT_PROJ, 512)], before_ref, outer_ref,
        lines_ref, right_lines_ref, left_ref, right_ref,
    )

    def sums_of(slot):
        return [
            outer_ref[pl.ds(slot * MAIN * WIDTH, MAIN * WIDTH), :],
            outer_ref[pl.ds((2 * MAIN + REST * slot) * WIDTH, REST * WIDTH), :],
        ]

    centred1, valid1 = split_lines(block_ref[...])
    half_gate1 = dot(centred1, weights_ref[:, pl.ds(OUT_GATE, 128)]) * scale_of(centred1)
    half_gate = jnp.concatenate([half_gate0_ref[...], half_gate1], axis=0)
    centred = jnp.concatenate([centred0_ref[...], centred1], axis=0)
    sums = centre(jnp.concatenate(sums_of(1) + sums_of(0), axis=0))
    change = gated(half_gate, dot(sums, weights_ref[:, pl.ds(OUT_FINAL, 128)]) * scale_of(sums))
    mid = centre(centred + change)
    scale = scale_of(mid)
    change_ref[...] = change[:LENGTH]
    normed_ref[...] = mid[:LENGTH] * scale[:LENGTH]
    proj = dot(mid[:LENGTH], weights_ref[:, pl.ds(IN_PROJ + 256, 256)]) * scale[:LENGTH]
    right2_ref[...] = valid0_ref[...] * gated(proj[:, :128], proj[:, 128:])
    proj = dot(mid[LENGTH:], weights_ref[:, pl.ds(IN_PROJ, 256)]) * scale[LENGTH:]
    left2_ref[...] = jnp.where(valid1, gated(proj[:, :128], proj[:, 128:]), 0.0)

    for j in range(SIDE):
        right = right2_ref[pl.ds(j * WIDTH, WIDTH), :]
        for i in range(SIDE):
            product = left2_ref[pl.ds(i * WIDTH, WIDTH), :] * right
            folded = product[:8]
            for t in range(1, WIDTH // 8):
                folded = folded + product[8 * t : 8 * (t + 1)]
            at = MAIN * j + i if i < MAIN else rest_rows(i - MAIN) + j
            pieces_ref[pl.ds(8 * at, 8), :] = folded
    inner = pieces_ref[pl.ds(0, ROWS, stride=8), :]
    for t in range(1, 8):
        inner = inner + pieces_ref[pl.ds(t, ROWS, stride=8), :]

    def own_rows(source_ref, flat_ref):
        for k in range(SIDE):
            flat_ref[pl.ds(MAIN * k, MAIN), :] = source_ref[pl.ds(WIDTH * k, MAIN), :]
        for e in range(REST):
            flat_ref[pl.ds(rest_rows(e), SIDE), :] = source_ref[pl.ds(MAIN * SPLIT + e, SIDE, stride=WIDTH), :]
        return flat_ref[...]

    mid = own_ref[...] + own_rows(change_ref, flat_ref)
    half_gate = dot(own_rows(normed_ref, flat2_ref), weights_ref[:, pl.ds(IN_GATE, 128)])
    inner = centre(inner)
    result = mid + gated(half_gate, dot(inner, weights_ref[:, pl.ds(IN_FINAL, 128)]) * scale_of(inner))
    for k in range(SIDE):
        result_ref[pl.ds(0, MAIN), k, :] = result[MAIN * k : MAIN * (k + 1)]
        for e in range(REST):
            result_ref[MAIN + e, pl.ds(k, 1), :] = result[rest_rows(e) + k : rest_rows(e) + k + 1]


def swapped(value, rows, cols):
    pairs = [
        (r * SPLIT + c, (r ^ rows) * SPLIT + (c ^ cols)) for r in range(SPLIT) for c in range(SPLIT)
    ]
    return lax.ppermute(value, ("row", "col"), pairs)


STEPS = (1, 2, 3)


def shifted(value, step, cols=0):
    pairs = [
        (r * SPLIT + c, (r + step) % SPLIT * SPLIT + (c ^ cols)) for r in range(SPLIT) for c in range(SPLIT)
    ]
    return lax.ppermute(value, ("row", "col"), pairs)


def in_vmem(value):
    return pltpu.with_memory_space_constraint(value, pltpu.VMEM)


def call(kernel, name, cycles, out, scratch, *operands, grant=32 << 20, **more):
    return pl.pallas_call(
        kernel,
        out_shape=out,
        scratch_shapes=[pltpu.VMEM(one, jnp.float32) if isinstance(one, tuple) else one for one in scratch],
        cost_estimate=pl.CostEstimate(flops=cycles, bytes_accessed=0, transcendentals=0),
        compiler_params=pltpu.CompilerParams(vmem_limit_bytes=grant),
        name=name,
        **more,
    )(*operands)


def compact_plan(pair, pair_mask, *weights):
    f32 = jnp.float32
    tile, own = call(
        pack_kernel, "pack", 1000, (pltpu.VMEM((ROWS, 128), jnp.bfloat16), pltpu.VMEM((ROWS, 128), f32)),
        [(ROWS, 128), pair.shape, pltpu.VMEM(pair_mask.shape, jnp.int32), pltpu.SemaphoreType.DMA((2,))],
        pair, pair_mask, grant=None, in_specs=2 * [pl.BlockSpec(memory_space=pl.ANY)],
    )
    around = [tile] + [shifted(tile, step) for step in STEPS]
    aslant = shifted(tile, STEPS[2], 2)
    early = jnp.stack(around[:3])
    swapped_early = swapped(early, 0, 2)
    late, _ = lax.optimization_barrier((around[3], early))
    part0 = jnp.concatenate([early, late[None]])
    lines = pltpu.VMEM((LENGTH, 128), f32)
    sums = pltpu.VMEM((2 * LENGTH, 128), f32)
    work = [(LENGTH, 128), (SIDE * RIGHT_LINE, 128), (LENGTH, 128), (SIDE * RIGHT_LINE, 128)]
    cost = 1 << 10
    outer = call(first_kernel, "first", cost, sums, work, in_vmem(part0), in_vmem(weights[0]))
    outer, *weights = lax.optimization_barrier((outer, *weights))
    weights = call(
        weights_kernel, "weights", 1000, pltpu.VMEM((2 * 128, WEIGHTS), jnp.bfloat16), [], *weights, grant=None
    )
    aslant, swapped_early, outer, weights = lax.optimization_barrier((aslant, swapped_early, outer, weights))
    part2 = jnp.concatenate([swapped_early, aslant[None]])
    weights = in_vmem(weights)
    part1 = swapped(part0, 0, 1)
    outer, centred0, gate0, valid0 = call(
        gate_kernel, "second", cost, (sums, lines, lines, lines), work + [(LENGTH, 128)],
        *map(in_vmem, (part1, part0, own)), weights, in_vmem(outer),
    )
    part3 = swapped(part2, 0, 1)
    outer = call(next_kernel, "third", cost, sums, work, in_vmem(part2), weights, in_vmem(outer))
    part3, outer = lax.optimization_barrier((part3, outer))
    return call(
        last_kernel, "last", cost, jax.ShapeDtypeStruct(pair.shape, f32),
        work + [(2 * LENGTH, 128)] + 5 * [(LENGTH, 128)] + [(8 * ROWS, 128), (ROWS, 128), (ROWS, 128)],
        *map(in_vmem, (part0, part1, part2, part3, outer, centred0, gate0, valid0, own)),
        weights,
    )


def solution(mesh):
    def body(pair, *rest):
        compact = (
            mesh.shape["row"] == mesh.shape["col"] == SPLIT
            and pair.shape == (SIDE, SIDE, 128)
            and rest[1].shape == (128, 512)
        )
        return (compact_plan if compact else split_plan)(pair, *rest)

    return jax.shard_map(
        body,
        mesh=mesh,
        in_specs=(
            P(("grp", "row"), "col", None),
            P(("grp", "row"), "col"),
            P(),
            P(),
            P(),
            P(),
            P(),
            P(),
        ),
        out_specs=P(("grp", "row"), "col", None),
        check_vma=False,
    )
```

```python
import jax
import jax.numpy as jnp
from jax import lax
from jax.experimental import pallas as pl
from jax.experimental.pallas import tpu as pltpu
from jax.sharding import PartitionSpec as P

MASKED = 64.0
SPLIT = 4
SIDE = 10
MAIN = 8
REST = SIDE - MAIN
ROWS = 112
WIDTH = SIDE * SPLIT


def layer_norm(value):
    mean = jnp.mean(value, axis=-1, keepdims=True)
    centred = value - mean
    variance = jnp.mean(centred * centred, axis=-1, keepdims=True)
    return centred * lax.rsqrt(variance + 1e-05)


def project(pair, pair_mask, proj_weight, gate_weight):
    normed = layer_norm(pair)
    proj = jnp.einsum("ijc,cd->ijd", normed, proj_weight, precision=lax.Precision.HIGHEST)
    hidden = proj_weight.shape[1] // 4
    valid = pair_mask.astype(jnp.float32)[:, :, None]
    left = jax.nn.sigmoid(proj[..., :hidden]) * proj[..., hidden : 2 * hidden] * valid
    right = jax.nn.sigmoid(proj[..., 2 * hidden : 3 * hidden]) * proj[..., 3 * hidden :] * valid
    gate = jax.nn.sigmoid(
        jnp.einsum("ijc,cd->ijd", normed, gate_weight, precision=lax.Precision.HIGHEST)
    )
    left = jnp.transpose(left.astype(jnp.bfloat16), (2, 0, 1))
    right = jnp.transpose(right.astype(jnp.bfloat16), (2, 0, 1))
    return (left, right, gate)


def finish(pair, summed, gate, final_weight):
    normed = layer_norm(jnp.transpose(summed, (1, 2, 0)))
    return pair + gate * jnp.einsum(
        "ijh,hc->ijc", normed, final_weight, precision=lax.Precision.HIGHEST
    )


def split_plan(pair, pair_mask, out_proj, out_gate, out_final, in_proj, in_gate, in_final):
    left, right, gate = project(pair, pair_mask, out_proj, out_gate)
    outer_terms = jnp.einsum(
        "hik,hjk->hij",
        left,
        lax.all_gather(right, "row", axis=1, tiled=True),
        preferred_element_type=jnp.float32,
    )
    outer = lax.psum_scatter(
        outer_terms.astype(jnp.bfloat16), "col", scatter_dimension=2, tiled=True
    ).astype(jnp.float32)
    middle = finish(pair, outer, gate, out_final)
    left2, right2, gate2 = project(middle, pair_mask, in_proj, in_gate)
    inner_terms = jnp.einsum(
        "hki,hkj->hij",
        lax.all_gather(left2, "col", axis=2, tiled=True),
        right2,
        preferred_element_type=jnp.float32,
    )
    inner = lax.psum_scatter(
        inner_terms.astype(jnp.bfloat16), "row", scatter_dimension=1, tiled=True
    ).astype(jnp.float32)
    return finish(middle, inner, gate2, in_final)


def gated(half_gate, half_value):
    return (jnp.tanh(half_gate) + 1.0) * half_value


def halved(weight):
    half = 0.5 * weight
    high = half.astype(jnp.bfloat16)
    low = (half - high.astype(jnp.float32)).astype(jnp.bfloat16)
    return jnp.concatenate([high, low], axis=0)


def dot(value, terms):
    value = value.astype(jnp.bfloat16)
    return jnp.dot(jnp.concatenate([value, value], axis=1), terms, preferred_element_type=jnp.float32)


def centre(value):
    return value - jnp.mean(value, axis=-1, keepdims=True)


def scale_of(centred):
    return lax.rsqrt(jnp.mean(centred * centred, axis=-1, keepdims=True) + 1e-05)


def rest_rows(k):
    return 80 + 16 * k


def pack_kernel(pair_ref, mask_ref, tile_ref, own_ref, valid_ref, pair_vmem, mask_vmem, sems):
    pair_copy = pltpu.make_async_copy(pair_ref, pair_vmem, sems.at[0])
    mask_copy = pltpu.make_async_copy(mask_ref, mask_vmem, sems.at[1])
    pair_copy.start()
    mask_copy.start()
    rest = pl.ds(MAIN * SIDE, ROWS - MAIN * SIDE)
    own_ref[rest, :] = jnp.zeros((ROWS - MAIN * SIDE, 128), own_ref.dtype)
    valid_ref[rest, :] = jnp.zeros((ROWS - MAIN * SIDE, 128), valid_ref.dtype)
    mask_copy.wait()
    valid = mask_vmem[...].astype(jnp.float32)
    for k in range(SIDE):
        column = jnp.broadcast_to(valid[:, k : k + 1], (SIDE, 128))
        valid_ref[pl.ds(MAIN * k, MAIN), :] = column[:MAIN]
        for e in range(REST):
            valid_ref[pl.ds(rest_rows(e) + k, 1), :] = column[MAIN + e : MAIN + e + 1]
    pair_copy.wait()
    for i in range(SIDE):
        at = pl.ds(i, SIDE, stride=MAIN) if i < MAIN else pl.ds(rest_rows(i - MAIN), SIDE)
        own_ref[at, :] = pair_vmem[i]
    own = own_ref[...]
    centred = own - jnp.mean(own, axis=-1, keepdims=True)
    tile_ref[...] = jnp.where(valid_ref[...] > 0.5, centred, MASKED).astype(tile_ref.dtype)


OUT_PROJ, OUT_GATE, OUT_FINAL, IN_PROJ, IN_GATE, IN_FINAL, WEIGHTS = 0, 512, 640, 768, 1280, 1408, 1536


def weights_kernel(*refs):
    start = 0
    for weight_ref in refs[:-1]:
        width = weight_ref.shape[1]
        refs[-1][:, pl.ds(start, width)] = halved(weight_ref[...])
        start += width


def to_lines(target, base, tile, slot, slots, line):
    for k in range(SIDE):
        target[pl.ds(base + line * k + MAIN * slot, MAIN), :] = tile[MAIN * k : MAIN * (k + 1)]
    for e in range(REST):
        target[pl.ds(base + MAIN * slots + REST * slot + e, SIDE, stride=line), :] = tile[
            rest_rows(e) : rest_rows(e) + SIDE
        ]


RIGHT_LINE = 24
LENGTH = SIDE * WIDTH
GROUP = 4


def add_terms(tiles, other, proj_weight, before_ref, outer_ref, lines_ref, right_lines_ref, left_ref, right_ref):
    for slot in range(SPLIT):
        to_lines(lines_ref, 0, tiles[slot].astype(jnp.float32), slot, SPLIT, WIDTH)
    to_lines(right_lines_ref, 0, tiles[0].astype(jnp.float32), 0, 2, RIGHT_LINE)
    to_lines(right_lines_ref, 0, tiles[other].astype(jnp.float32), 1, 2, RIGHT_LINE)
    raw = jnp.concatenate([lines_ref[...], right_lines_ref[...]], axis=0)
    centred = split_lines(raw)[0]
    scale = scale_of(centred)
    proj = dot(centred[:LENGTH], proj_weight[:, :256]) * scale[:LENGTH]
    left_ref[...] = gated(proj[:, :128], proj[:, 128:])
    proj = dot(centred[LENGTH:], proj_weight[:, 256:]) * scale[LENGTH:]
    right_ref[...] = gated(proj[:, :128], proj[:, 128:])

    for g in range(2 * SIDE // GROUP):
        at = [pl.ds((g * GROUP + t) * WIDTH, WIDTH) for t in range(GROUP)]
        sums = [None if before_ref is None else before_ref[at[t], :] for t in range(GROUP)]
        for k in range(SIDE):
            rows = left_ref[pl.ds(k * WIDTH, WIDTH), :]
            for t in range(GROUP):
                one = right_ref[pl.ds(k * RIGHT_LINE + g * GROUP + t, 1), :]
                term = rows * jnp.broadcast_to(one, rows.shape)
                sums[t] = term if sums[t] is None else sums[t] + term
        for t in range(GROUP):
            outer_ref[at[t], :] = sums[t]


def split_lines(raw):
    valid = raw < 0.5 * MASKED
    return jnp.where(valid, raw, 0.0), valid


def other_slot():
    before = lax.rem(lax.axis_index("row") - lax.axis_index("col") + SPLIT, SPLIT)
    place = jnp.int32(0)
    for number, step in enumerate(STEPS):
        place = jnp.where(before == step, number + 1, place)
    return place


def other_part():
    return jnp.bitwise_xor(lax.axis_index("row"), lax.axis_index("col"))


def first_kernel(tiles, out_proj_ref, outer_ref, *scratch):
    add_terms(tiles, other_slot(), halved(out_proj_ref[...]), None, outer_ref, *scratch)


def next_kernel(tiles, weights_ref, before_ref, outer_ref, *scratch):
    add_terms(tiles, other_slot(), weights_ref[:, pl.ds(OUT_PROJ, 512)], before_ref, outer_ref, *scratch)


def gate_kernel(tiles, own_tiles, own_ref, weights_ref, before_ref, outer_ref, centred_ref, half_gate_ref, valid_ref, *scratch):
    add_terms(tiles, other_slot(), weights_ref[:, pl.ds(OUT_PROJ, 512)], before_ref, outer_ref, *scratch[:-1])
    lines_ref = scratch[-1]
    for slot in range(SPLIT):
        to_lines(lines_ref, 0, own_tiles[slot].astype(jnp.float32), slot, SPLIT, WIDTH)
    centred, valid = split_lines(lines_ref[...])
    centred_ref[...] = centred
    valid_ref[...] = jnp.where(valid, 1.0, 0.0)
    own = own_ref[...]
    own = own - jnp.mean(own, axis=-1, keepdims=True)
    to_lines(centred_ref, 0, own, 0, SPLIT, WIDTH)
    centred = centred_ref[...]
    half_gate_ref[...] = dot(centred, weights_ref[:, pl.ds(OUT_GATE, 128)]) * scale_of(centred)


def last_kernel(
    part0, part1, part2, part3, before_ref, centred0_ref, half_gate0_ref, valid0_ref, own_ref,
    weights_ref,
    result_ref,
    lines_ref, right_lines_ref, left_ref, right_ref, outer_ref, block_ref, left2_ref, right2_ref, change_ref, normed_ref,
    pieces_ref, flat_ref, flat2_ref,
):
    for number, tiles in enumerate((part0, part1, part3, part2)):
        @pl.when(other_part() == number)
        def _():
            for slot in range(SPLIT):
                to_lines(block_ref, 0, tiles[slot].astype(jnp.float32), slot, SPLIT, WIDTH)

    add_terms(
        part3, other_slot(), weights_ref[:, pl.ds(OUT_PROJ, 512)], before_ref, outer_ref,
        lines_ref, right_lines_ref, left_ref, right_ref,
    )

    def sums_of(slot):
        return [
            outer_ref[pl.ds(slot * MAIN * WIDTH, MAIN * WIDTH), :],
            outer_ref[pl.ds((2 * MAIN + REST * slot) * WIDTH, REST * WIDTH), :],
        ]

    centred1, valid1 = split_lines(block_ref[...])
    half_gate1 = dot(centred1, weights_ref[:, pl.ds(OUT_GATE, 128)]) * scale_of(centred1)
    half_gate = jnp.concatenate([half_gate0_ref[...], half_gate1], axis=0)
    centred = jnp.concatenate([centred0_ref[...], centred1], axis=0)
    sums = centre(jnp.concatenate(sums_of(1) + sums_of(0), axis=0))
    change = gated(half_gate, dot(sums, weights_ref[:, pl.ds(OUT_FINAL, 128)]) * scale_of(sums))
    mid = centre(centred + change)
    scale = scale_of(mid)
    change_ref[...] = change[:LENGTH]
    normed_ref[...] = mid[:LENGTH] * scale[:LENGTH]
    proj = dot(mid[:LENGTH], weights_ref[:, pl.ds(IN_PROJ + 256, 256)]) * scale[:LENGTH]
    right2_ref[...] = valid0_ref[...] * gated(proj[:, :128], proj[:, 128:])
    proj = dot(mid[LENGTH:], weights_ref[:, pl.ds(IN_PROJ, 256)]) * scale[LENGTH:]
    left2_ref[...] = jnp.where(valid1, gated(proj[:, :128], proj[:, 128:]), 0.0)

    for j in range(SIDE):
        right = right2_ref[pl.ds(j * WIDTH, WIDTH), :]
        for i in range(SIDE):
            product = left2_ref[pl.ds(i * WIDTH, WIDTH), :] * right
            folded = product[:8]
            for t in range(1, WIDTH // 8):
                folded = folded + product[8 * t : 8 * (t + 1)]
            at = MAIN * j + i if i < MAIN else rest_rows(i - MAIN) + j
            pieces_ref[pl.ds(8 * at, 8), :] = folded
    inner = pieces_ref[pl.ds(0, ROWS, stride=8), :]
    for t in range(1, 8):
        inner = inner + pieces_ref[pl.ds(t, ROWS, stride=8), :]

    def own_rows(source_ref, flat_ref):
        for k in range(SIDE):
            flat_ref[pl.ds(MAIN * k, MAIN), :] = source_ref[pl.ds(WIDTH * k, MAIN), :]
        for e in range(REST):
            flat_ref[pl.ds(rest_rows(e), SIDE), :] = source_ref[pl.ds(MAIN * SPLIT + e, SIDE, stride=WIDTH), :]
        return flat_ref[...]

    mid = own_ref[...] + own_rows(change_ref, flat_ref)
    half_gate = dot(own_rows(normed_ref, flat2_ref), weights_ref[:, pl.ds(IN_GATE, 128)])
    inner = centre(inner)
    result = mid + gated(half_gate, dot(inner, weights_ref[:, pl.ds(IN_FINAL, 128)]) * scale_of(inner))
    for k in range(SIDE):
        result_ref[pl.ds(0, MAIN), k, :] = result[MAIN * k : MAIN * (k + 1)]
        for e in range(REST):
            result_ref[MAIN + e, pl.ds(k, 1), :] = result[rest_rows(e) + k : rest_rows(e) + k + 1]


def swapped(value, rows, cols):
    pairs = [
        (r * SPLIT + c, (r ^ rows) * SPLIT + (c ^ cols)) for r in range(SPLIT) for c in range(SPLIT)
    ]
    return lax.ppermute(value, ("row", "col"), pairs)


STEPS = (1, 2, 3)


def shifted(value, step, cols=0):
    pairs = [
        (r * SPLIT + c, (r + step) % SPLIT * SPLIT + (c ^ cols)) for r in range(SPLIT) for c in range(SPLIT)
    ]
    return lax.ppermute(value, ("row", "col"), pairs)


def in_vmem(value):
    return pltpu.with_memory_space_constraint(value, pltpu.VMEM)


def call(kernel, name, cycles, out, scratch, *operands, grant=32 << 20, **more):
    return pl.pallas_call(
        kernel,
        out_shape=out,
        scratch_shapes=[pltpu.VMEM(one, jnp.float32) if isinstance(one, tuple) else one for one in scratch],
        cost_estimate=pl.CostEstimate(flops=cycles, bytes_accessed=0, transcendentals=0),
        compiler_params=pltpu.CompilerParams(vmem_limit_bytes=grant),
        name=name,
        **more,
    )(*operands)


def compact_plan(pair, pair_mask, *weights):
    f32 = jnp.float32
    tile, own = call(
        pack_kernel, "pack", 1000, (pltpu.VMEM((ROWS, 128), jnp.bfloat16), pltpu.VMEM((ROWS, 128), f32)),
        [(ROWS, 128), pair.shape, pltpu.VMEM(pair_mask.shape, jnp.int32), pltpu.SemaphoreType.DMA((2,))],
        pair, pair_mask, grant=None, in_specs=2 * [pl.BlockSpec(memory_space=pl.ANY)],
    )
    around = [tile] + [shifted(tile, step) for step in STEPS]
    aslant = shifted(tile, STEPS[2], 3)
    early = jnp.stack(around[:3])
    swapped_early = swapped(early, 0, 3)
    late, _ = lax.optimization_barrier((around[3], early))
    part0 = jnp.concatenate([early, late[None]])
    lines = pltpu.VMEM((LENGTH, 128), f32)
    sums = pltpu.VMEM((2 * LENGTH, 128), f32)
    work = [(LENGTH, 128), (SIDE * RIGHT_LINE, 128), (LENGTH, 128), (SIDE * RIGHT_LINE, 128)]
    cost = 1 << 10
    outer = call(first_kernel, "first", cost, sums, work, in_vmem(part0), in_vmem(weights[0]))
    outer, *weights = lax.optimization_barrier((outer, *weights))
    weights = call(
        weights_kernel, "weights", 1000, pltpu.VMEM((2 * 128, WEIGHTS), jnp.bfloat16), [], *weights, grant=None
    )
    aslant, swapped_early, outer, weights = lax.optimization_barrier((aslant, swapped_early, outer, weights))
    part2 = jnp.concatenate([swapped_early, aslant[None]])
    weights = in_vmem(weights)
    part1 = swapped(part0, 0, 1)
    outer, centred0, gate0, valid0 = call(
        gate_kernel, "second", cost, (sums, lines, lines, lines), work + [(LENGTH, 128)],
        *map(in_vmem, (part1, part0, own)), weights, in_vmem(outer),
    )
    part3 = swapped(part2, 0, 1)
    outer = call(next_kernel, "third", cost, sums, work, in_vmem(part2), weights, in_vmem(outer))
    part3, outer = lax.optimization_barrier((part3, outer))
    return call(
        last_kernel, "last", cost, jax.ShapeDtypeStruct(pair.shape, f32),
        work + [(2 * LENGTH, 128)] + 5 * [(LENGTH, 128)] + [(8 * ROWS, 128), (ROWS, 128), (ROWS, 128)],
        *map(in_vmem, (part0, part1, part2, part3, outer, centred0, gate0, valid0, own)),
        weights,
    )


def solution(mesh):
    def body(pair, *rest):
        compact = (
            mesh.shape["row"] == mesh.shape["col"] == SPLIT
            and pair.shape == (SIDE, SIDE, 128)
            and rest[1].shape == (128, 512)
        )
        return (compact_plan if compact else split_plan)(pair, *rest)

    return jax.shard_map(
        body,
        mesh=mesh,
        in_specs=(
            P(("grp", "row"), "col", None),
            P(("grp", "row"), "col"),
            P(),
            P(),
            P(),
            P(),
            P(),
            P(),
        ),
        out_specs=P(("grp", "row"), "col", None),
        check_vma=False,
    )
```

```python
import jax
import jax.numpy as jnp
from jax import lax
from jax.experimental import pallas as pl
from jax.experimental.pallas import tpu as pltpu
from jax.sharding import PartitionSpec as P

MASKED = 64.0
SPLIT = 4
SIDE = 10
MAIN = 8
REST = SIDE - MAIN
ROWS = 112
WIDTH = SIDE * SPLIT


def layer_norm(value):
    mean = jnp.mean(value, axis=-1, keepdims=True)
    centred = value - mean
    variance = jnp.mean(centred * centred, axis=-1, keepdims=True)
    return centred * lax.rsqrt(variance + 1e-05)


def project(pair, pair_mask, proj_weight, gate_weight):
    normed = layer_norm(pair)
    proj = jnp.einsum("ijc,cd->ijd", normed, proj_weight, precision=lax.Precision.HIGHEST)
    hidden = proj_weight.shape[1] // 4
    valid = pair_mask.astype(jnp.float32)[:, :, None]
    left = jax.nn.sigmoid(proj[..., :hidden]) * proj[..., hidden : 2 * hidden] * valid
    right = jax.nn.sigmoid(proj[..., 2 * hidden : 3 * hidden]) * proj[..., 3 * hidden :] * valid
    gate = jax.nn.sigmoid(
        jnp.einsum("ijc,cd->ijd", normed, gate_weight, precision=lax.Precision.HIGHEST)
    )
    left = jnp.transpose(left.astype(jnp.bfloat16), (2, 0, 1))
    right = jnp.transpose(right.astype(jnp.bfloat16), (2, 0, 1))
    return (left, right, gate)


def finish(pair, summed, gate, final_weight):
    normed = layer_norm(jnp.transpose(summed, (1, 2, 0)))
    return pair + gate * jnp.einsum(
        "ijh,hc->ijc", normed, final_weight, precision=lax.Precision.HIGHEST
    )


def split_plan(pair, pair_mask, out_proj, out_gate, out_final, in_proj, in_gate, in_final):
    left, right, gate = project(pair, pair_mask, out_proj, out_gate)
    outer_terms = jnp.einsum(
        "hik,hjk->hij",
        left,
        lax.all_gather(right, "row", axis=1, tiled=True),
        preferred_element_type=jnp.float32,
    )
    outer = lax.psum_scatter(
        outer_terms.astype(jnp.bfloat16), "col", scatter_dimension=2, tiled=True
    ).astype(jnp.float32)
    middle = finish(pair, outer, gate, out_final)
    left2, right2, gate2 = project(middle, pair_mask, in_proj, in_gate)
    inner_terms = jnp.einsum(
        "hki,hkj->hij",
        lax.all_gather(left2, "col", axis=2, tiled=True),
        right2,
        preferred_element_type=jnp.float32,
    )
    inner = lax.psum_scatter(
        inner_terms.astype(jnp.bfloat16), "row", scatter_dimension=1, tiled=True
    ).astype(jnp.float32)
    return finish(middle, inner, gate2, in_final)


def gated(half_gate, half_value):
    return (jnp.tanh(half_gate) + 1.0) * half_value


def halved(weight):
    half = 0.5 * weight
    high = half.astype(jnp.bfloat16)
    low = (half - high.astype(jnp.float32)).astype(jnp.bfloat16)
    return jnp.concatenate([high, low], axis=0)


def dot(value, terms):
    value = value.astype(jnp.bfloat16)
    return jnp.dot(jnp.concatenate([value, value], axis=1), terms, preferred_element_type=jnp.float32)


def centre(value):
    return value - jnp.mean(value, axis=-1, keepdims=True)


def scale_of(centred):
    return lax.rsqrt(jnp.mean(centred * centred, axis=-1, keepdims=True) + 1e-05)


def scale_of_whole(value):
    mean = jnp.mean(value, axis=-1, keepdims=True)
    square = jnp.mean(value * value, axis=-1, keepdims=True)
    return lax.rsqrt(jnp.maximum(square - mean * mean, 0.0) + 1e-05)


def rest_rows(k):
    return 80 + 16 * k


def pack_kernel(pair_ref, mask_ref, tile_ref, own_ref, valid_ref, pair_vmem, mask_vmem, sems):
    pair_copy = pltpu.make_async_copy(pair_ref, pair_vmem, sems.at[0])
    mask_copy = pltpu.make_async_copy(mask_ref, mask_vmem, sems.at[1])
    pair_copy.start()
    mask_copy.start()
    rest = pl.ds(MAIN * SIDE, ROWS - MAIN * SIDE)
    own_ref[rest, :] = jnp.zeros((ROWS - MAIN * SIDE, 128), own_ref.dtype)
    valid_ref[rest, :] = jnp.zeros((ROWS - MAIN * SIDE, 128), valid_ref.dtype)
    mask_copy.wait()
    valid = mask_vmem[...].astype(jnp.float32)
    for k in range(SIDE):
        column = jnp.broadcast_to(valid[:, k : k + 1], (SIDE, 128))
        valid_ref[pl.ds(MAIN * k, MAIN), :] = column[:MAIN]
        for e in range(REST):
            valid_ref[pl.ds(rest_rows(e) + k, 1), :] = column[MAIN + e : MAIN + e + 1]
    pair_copy.wait()
    for i in range(SIDE):
        at = pl.ds(i, SIDE, stride=MAIN) if i < MAIN else pl.ds(rest_rows(i - MAIN), SIDE)
        own_ref[at, :] = pair_vmem[i]
    own = own_ref[...]
    centred = own - jnp.mean(own, axis=-1, keepdims=True)
    tile_ref[...] = jnp.where(valid_ref[...] > 0.5, centred, MASKED).astype(tile_ref.dtype)


OUT_PROJ, OUT_GATE, OUT_FINAL, IN_PROJ, IN_GATE, IN_FINAL, WEIGHTS = 0, 512, 640, 768, 1280, 1408, 1536


def weights_kernel(*refs):
    start = 0
    for weight_ref in refs[:-1]:
        weight, width = weight_ref[...], weight_ref.shape[1]
        if start in (IN_PROJ, IN_GATE):
            weight = weight - jnp.mean(weight, axis=0, keepdims=True)
        refs[-1][:, pl.ds(start, width)] = halved(weight)
        start += width


def to_lines(target, base, tile, slot, slots, line):
    for k in range(SIDE):
        target[pl.ds(base + line * k + MAIN * slot, MAIN), :] = tile[MAIN * k : MAIN * (k + 1)]
    for e in range(REST):
        target[pl.ds(base + MAIN * slots + REST * slot + e, SIDE, stride=line), :] = tile[
            rest_rows(e) : rest_rows(e) + SIDE
        ]


RIGHT_LINE = 24
LENGTH = SIDE * WIDTH
GROUP = 4


def add_terms(tiles, other, proj_weight, before_ref, outer_ref, lines_ref, right_lines_ref, left_ref, right_ref):
    for slot in range(SPLIT):
        to_lines(lines_ref, 0, tiles[slot].astype(jnp.float32), slot, SPLIT, WIDTH)
    to_lines(right_lines_ref, 0, tiles[0].astype(jnp.float32), 0, 2, RIGHT_LINE)
    to_lines(right_lines_ref, 0, tiles[other].astype(jnp.float32), 1, 2, RIGHT_LINE)
    raw = jnp.concatenate([lines_ref[...], right_lines_ref[...]], axis=0)
    centred = split_lines(raw)[0]
    scale = scale_of(centred)
    proj = dot(centred[:LENGTH], proj_weight[:, :256]) * scale[:LENGTH]
    left_ref[...] = gated(proj[:, :128], proj[:, 128:])
    proj = dot(centred[LENGTH:], proj_weight[:, 256:]) * scale[LENGTH:]
    right_ref[...] = gated(proj[:, :128], proj[:, 128:])

    for g in range(2 * SIDE // GROUP):
        at = [pl.ds((g * GROUP + t) * WIDTH, WIDTH) for t in range(GROUP)]
        sums = [None if before_ref is None else before_ref[at[t], :] for t in range(GROUP)]
        for k in range(SIDE):
            rows = left_ref[pl.ds(k * WIDTH, WIDTH), :]
            for t in range(GROUP):
                one = right_ref[pl.ds(k * RIGHT_LINE + g * GROUP + t, 1), :]
                term = rows * jnp.broadcast_to(one, rows.shape)
                sums[t] = term if sums[t] is None else sums[t] + term
        for t in range(GROUP):
            outer_ref[at[t], :] = sums[t]


def split_lines(raw):
    valid = raw < 0.5 * MASKED
    return jnp.where(valid, raw, 0.0), valid


def other_slot():
    before = lax.rem(lax.axis_index("row") - lax.axis_index("col") + SPLIT, SPLIT)
    place = jnp.int32(0)
    for number, step in enumerate(STEPS):
        place = jnp.where(before == step, number + 1, place)
    return place


def other_part():
    return jnp.bitwise_xor(lax.axis_index("row"), lax.axis_index("col"))


def first_kernel(tiles, out_proj_ref, outer_ref, *scratch):
    add_terms(tiles, other_slot(), halved(out_proj_ref[...]), None, outer_ref, *scratch)


def next_kernel(tiles, weights_ref, before_ref, outer_ref, *scratch):
    add_terms(tiles, other_slot(), weights_ref[:, pl.ds(OUT_PROJ, 512)], before_ref, outer_ref, *scratch)


def gate_kernel(tiles, own_tiles, own_ref, weights_ref, before_ref, outer_ref, centred_ref, half_gate_ref, valid_ref, *scratch):
    add_terms(tiles, other_slot(), weights_ref[:, pl.ds(OUT_PROJ, 512)], before_ref, outer_ref, *scratch[:-1])
    lines_ref = scratch[-1]
    for slot in range(SPLIT):
        to_lines(lines_ref, 0, own_tiles[slot].astype(jnp.float32), slot, SPLIT, WIDTH)
    centred, valid = split_lines(lines_ref[...])
    centred_ref[...] = centred
    valid_ref[...] = jnp.where(valid, 1.0, 0.0)
    own = own_ref[...]
    own = own - jnp.mean(own, axis=-1, keepdims=True)
    to_lines(centred_ref, 0, own, 0, SPLIT, WIDTH)
    centred = centred_ref[...]
    half_gate_ref[...] = dot(centred, weights_ref[:, pl.ds(OUT_GATE, 128)]) * scale_of(centred)


def last_kernel(
    part0, part1, part2, part3, before_ref, centred0_ref, half_gate0_ref, valid0_ref, own_ref,
    weights_ref,
    result_ref,
    lines_ref, right_lines_ref, left_ref, right_ref, outer_ref, block_ref, left2_ref, right2_ref, change_ref, normed_ref,
    pieces_ref, flat_ref, flat2_ref,
):
    for number, tiles in enumerate((part0, part1, part3, part2)):
        @pl.when(other_part() == number)
        def _():
            for slot in range(SPLIT):
                to_lines(block_ref, 0, tiles[slot].astype(jnp.float32), slot, SPLIT, WIDTH)

    add_terms(
        part3, other_slot(), weights_ref[:, pl.ds(OUT_PROJ, 512)], before_ref, outer_ref,
        lines_ref, right_lines_ref, left_ref, right_ref,
    )

    def sums_of(slot):
        return [
            outer_ref[pl.ds(slot * MAIN * WIDTH, MAIN * WIDTH), :],
            outer_ref[pl.ds((2 * MAIN + REST * slot) * WIDTH, REST * WIDTH), :],
        ]

    centred1, valid1 = split_lines(block_ref[...])
    half_gate1 = dot(centred1, weights_ref[:, pl.ds(OUT_GATE, 128)]) * scale_of(centred1)
    half_gate = jnp.concatenate([half_gate0_ref[...], half_gate1], axis=0)
    centred = jnp.concatenate([centred0_ref[...], centred1], axis=0)
    sums = centre(jnp.concatenate(sums_of(1) + sums_of(0), axis=0))
    change = gated(half_gate, dot(sums, weights_ref[:, pl.ds(OUT_FINAL, 128)]) * scale_of(sums))
    mid = centred + change
    scale = scale_of_whole(mid)
    change_ref[...] = change[:LENGTH]
    normed_ref[...] = mid[:LENGTH] * scale[:LENGTH]
    proj = dot(mid[:LENGTH], weights_ref[:, pl.ds(IN_PROJ + 256, 256)]) * scale[:LENGTH]
    right2_ref[...] = valid0_ref[...] * gated(proj[:, :128], proj[:, 128:])
    proj = dot(mid[LENGTH:], weights_ref[:, pl.ds(IN_PROJ, 256)]) * scale[LENGTH:]
    left2_ref[...] = jnp.where(valid1, gated(proj[:, :128], proj[:, 128:]), 0.0)

    for j in range(SIDE):
        right = right2_ref[pl.ds(j * WIDTH, WIDTH), :]
        for i in range(SIDE):
            product = left2_ref[pl.ds(i * WIDTH, WIDTH), :] * right
            folded = product[:8]
            for t in range(1, WIDTH // 8):
                folded = folded + product[8 * t : 8 * (t + 1)]
            at = MAIN * j + i if i < MAIN else rest_rows(i - MAIN) + j
            pieces_ref[pl.ds(8 * at, 8), :] = folded
    inner = pieces_ref[pl.ds(0, ROWS, stride=8), :]
    for t in range(1, 8):
        inner = inner + pieces_ref[pl.ds(t, ROWS, stride=8), :]

    def own_rows(source_ref, flat_ref):
        for k in range(SIDE):
            flat_ref[pl.ds(MAIN * k, MAIN), :] = source_ref[pl.ds(WIDTH * k, MAIN), :]
        for e in range(REST):
            flat_ref[pl.ds(rest_rows(e), SIDE), :] = source_ref[pl.ds(MAIN * SPLIT + e, SIDE, stride=WIDTH), :]
        return flat_ref[...]

    mid = own_ref[...] + own_rows(change_ref, flat_ref)
    half_gate = dot(own_rows(normed_ref, flat2_ref), weights_ref[:, pl.ds(IN_GATE, 128)])
    inner = centre(inner)
    result = mid + gated(half_gate, dot(inner, weights_ref[:, pl.ds(IN_FINAL, 128)]) * scale_of(inner))
    for k in range(SIDE):
        result_ref[pl.ds(0, MAIN), k, :] = result[MAIN * k : MAIN * (k + 1)]
        for e in range(REST):
            result_ref[MAIN + e, pl.ds(k, 1), :] = result[rest_rows(e) + k : rest_rows(e) + k + 1]


def swapped(value, rows, cols):
    pairs = [
        (r * SPLIT + c, (r ^ rows) * SPLIT + (c ^ cols)) for r in range(SPLIT) for c in range(SPLIT)
    ]
    return lax.ppermute(value, ("row", "col"), pairs)


STEPS = (1, 2, 3)


def shifted(value, step, cols=0):
    pairs = [
        (r * SPLIT + c, (r + step) % SPLIT * SPLIT + (c ^ cols)) for r in range(SPLIT) for c in range(SPLIT)
    ]
    return lax.ppermute(value, ("row", "col"), pairs)


def in_vmem(value):
    return pltpu.with_memory_space_constraint(value, pltpu.VMEM)


def call(kernel, name, cycles, out, scratch, *operands, grant=32 << 20, **more):
    return pl.pallas_call(
        kernel,
        out_shape=out,
        scratch_shapes=[pltpu.VMEM(one, jnp.float32) if isinstance(one, tuple) else one for one in scratch],
        cost_estimate=pl.CostEstimate(flops=cycles, bytes_accessed=0, transcendentals=0),
        compiler_params=pltpu.CompilerParams(vmem_limit_bytes=grant),
        name=name,
        **more,
    )(*operands)


def compact_plan(pair, pair_mask, *weights):
    f32 = jnp.float32
    tile, own = call(
        pack_kernel, "pack", 1000, (pltpu.VMEM((ROWS, 128), jnp.bfloat16), pltpu.VMEM((ROWS, 128), f32)),
        [(ROWS, 128), pair.shape, pltpu.VMEM(pair_mask.shape, jnp.int32), pltpu.SemaphoreType.DMA((2,))],
        pair, pair_mask, grant=None, in_specs=2 * [pl.BlockSpec(memory_space=pl.ANY)],
    )
    around = [tile] + [shifted(tile, step) for step in STEPS]
    aslant = shifted(tile, STEPS[2], 3)
    early = jnp.stack(around[:3])
    swapped_early = swapped(early, 0, 3)
    late, _ = lax.optimization_barrier((around[3], early))
    part0 = jnp.concatenate([early, late[None]])
    lines = pltpu.VMEM((LENGTH, 128), f32)
    sums = pltpu.VMEM((2 * LENGTH, 128), f32)
    work = [(LENGTH, 128), (SIDE * RIGHT_LINE, 128), (LENGTH, 128), (SIDE * RIGHT_LINE, 128)]
    cost = 1 << 10
    outer = call(first_kernel, "first", cost, sums, work, in_vmem(part0), in_vmem(weights[0]))
    outer, *weights = lax.optimization_barrier((outer, *weights))
    weights = call(
        weights_kernel, "weights", 1000, pltpu.VMEM((2 * 128, WEIGHTS), jnp.bfloat16), [], *weights, grant=None
    )
    aslant, swapped_early, outer, weights = lax.optimization_barrier((aslant, swapped_early, outer, weights))
    part2 = jnp.concatenate([swapped_early, aslant[None]])
    weights = in_vmem(weights)
    part1 = swapped(part0, 0, 1)
    outer, centred0, gate0, valid0 = call(
        gate_kernel, "second", cost, (sums, lines, lines, lines), work + [(LENGTH, 128)],
        *map(in_vmem, (part1, part0, own)), weights, in_vmem(outer),
    )
    part3 = swapped(part2, 0, 1)
    outer = call(next_kernel, "third", cost, sums, work, in_vmem(part2), weights, in_vmem(outer))
    part3, outer = lax.optimization_barrier((part3, outer))
    return call(
        last_kernel, "last", cost, jax.ShapeDtypeStruct(pair.shape, f32),
        work + [(2 * LENGTH, 128)] + 5 * [(LENGTH, 128)] + [(8 * ROWS, 128), (ROWS, 128), (ROWS, 128)],
        *map(in_vmem, (part0, part1, part2, part3, outer, centred0, gate0, valid0, own)),
        weights,
    )


def solution(mesh):
    def body(pair, *rest):
        compact = (
            mesh.shape["row"] == mesh.shape["col"] == SPLIT
            and pair.shape == (SIDE, SIDE, 128)
            and rest[1].shape == (128, 512)
        )
        return (compact_plan if compact else split_plan)(pair, *rest)

    return jax.shard_map(
        body,
        mesh=mesh,
        in_specs=(
            P(("grp", "row"), "col", None),
            P(("grp", "row"), "col"),
            P(),
            P(),
            P(),
            P(),
            P(),
            P(),
        ),
        out_specs=P(("grp", "row"), "col", None),
        check_vma=False,
    )
```

```python
import jax
import jax.numpy as jnp
from jax import lax
from jax.experimental import pallas as pl
from jax.experimental.pallas import tpu as pltpu
from jax.sharding import PartitionSpec as P

MASKED = 64.0
SPLIT = 4
SIDE = 10
MAIN = 8
REST = SIDE - MAIN
ROWS = 112
WIDTH = SIDE * SPLIT


def layer_norm(value):
    mean = jnp.mean(value, axis=-1, keepdims=True)
    centred = value - mean
    variance = jnp.mean(centred * centred, axis=-1, keepdims=True)
    return centred * lax.rsqrt(variance + 1e-05)


def project(pair, pair_mask, proj_weight, gate_weight):
    normed = layer_norm(pair)
    proj = jnp.einsum("ijc,cd->ijd", normed, proj_weight, precision=lax.Precision.HIGHEST)
    hidden = proj_weight.shape[1] // 4
    valid = pair_mask.astype(jnp.float32)[:, :, None]
    left = jax.nn.sigmoid(proj[..., :hidden]) * proj[..., hidden : 2 * hidden] * valid
    right = jax.nn.sigmoid(proj[..., 2 * hidden : 3 * hidden]) * proj[..., 3 * hidden :] * valid
    gate = jax.nn.sigmoid(
        jnp.einsum("ijc,cd->ijd", normed, gate_weight, precision=lax.Precision.HIGHEST)
    )
    left = jnp.transpose(left.astype(jnp.bfloat16), (2, 0, 1))
    right = jnp.transpose(right.astype(jnp.bfloat16), (2, 0, 1))
    return (left, right, gate)


def finish(pair, summed, gate, final_weight):
    normed = layer_norm(jnp.transpose(summed, (1, 2, 0)))
    return pair + gate * jnp.einsum(
        "ijh,hc->ijc", normed, final_weight, precision=lax.Precision.HIGHEST
    )


def split_plan(pair, pair_mask, out_proj, out_gate, out_final, in_proj, in_gate, in_final):
    left, right, gate = project(pair, pair_mask, out_proj, out_gate)
    outer_terms = jnp.einsum(
        "hik,hjk->hij",
        left,
        lax.all_gather(right, "row", axis=1, tiled=True),
        preferred_element_type=jnp.float32,
    )
    outer = lax.psum_scatter(
        outer_terms.astype(jnp.bfloat16), "col", scatter_dimension=2, tiled=True
    ).astype(jnp.float32)
    middle = finish(pair, outer, gate, out_final)
    left2, right2, gate2 = project(middle, pair_mask, in_proj, in_gate)
    inner_terms = jnp.einsum(
        "hki,hkj->hij",
        lax.all_gather(left2, "col", axis=2, tiled=True),
        right2,
        preferred_element_type=jnp.float32,
    )
    inner = lax.psum_scatter(
        inner_terms.astype(jnp.bfloat16), "row", scatter_dimension=1, tiled=True
    ).astype(jnp.float32)
    return finish(middle, inner, gate2, in_final)


def gated(half_gate, half_value):
    return (jnp.tanh(half_gate) + 1.0) * half_value


def halved(weight):
    half = 0.5 * weight
    high = half.astype(jnp.bfloat16)
    low = (half - high.astype(jnp.float32)).astype(jnp.bfloat16)
    return jnp.concatenate([high, low], axis=0)


def dot(value, terms):
    value = value.astype(jnp.bfloat16)
    return jnp.dot(jnp.concatenate([value, value], axis=1), terms, preferred_element_type=jnp.float32)


def centre(value):
    return value - jnp.mean(value, axis=-1, keepdims=True)


def scale_of(centred):
    return lax.rsqrt(jnp.mean(centred * centred, axis=-1, keepdims=True) + 1e-05)


def scale_of_whole(value):
    mean = jnp.mean(value, axis=-1, keepdims=True)
    square = jnp.mean(value * value, axis=-1, keepdims=True)
    return lax.rsqrt(jnp.maximum(square - mean * mean, 0.0) + 1e-05)


def rest_rows(k):
    return 80 + 16 * k


def pack_kernel(pair_ref, mask_ref, tile_ref, own_ref, valid_ref, pair_vmem, mask_vmem, sems):
    pair_copy = pltpu.make_async_copy(pair_ref, pair_vmem, sems.at[0])
    mask_copy = pltpu.make_async_copy(mask_ref, mask_vmem, sems.at[1])
    pair_copy.start()
    mask_copy.start()
    rest = pl.ds(MAIN * SIDE, ROWS - MAIN * SIDE)
    own_ref[rest, :] = jnp.zeros((ROWS - MAIN * SIDE, 128), own_ref.dtype)
    valid_ref[rest, :] = jnp.zeros((ROWS - MAIN * SIDE, 128), valid_ref.dtype)
    mask_copy.wait()
    valid = mask_vmem[...].astype(jnp.float32)
    for k in range(SIDE):
        column = jnp.broadcast_to(valid[:, k : k + 1], (SIDE, 128))
        valid_ref[pl.ds(MAIN * k, MAIN), :] = column[:MAIN]
        for e in range(REST):
            valid_ref[pl.ds(rest_rows(e) + k, 1), :] = column[MAIN + e : MAIN + e + 1]
    pair_copy.wait()
    for i in range(SIDE):
        at = pl.ds(i, SIDE, stride=MAIN) if i < MAIN else pl.ds(rest_rows(i - MAIN), SIDE)
        own_ref[at, :] = pair_vmem[i]
    own = own_ref[...]
    centred = own - jnp.mean(own, axis=-1, keepdims=True)
    tile_ref[...] = jnp.where(valid_ref[...] > 0.5, centred, MASKED).astype(tile_ref.dtype)


OUT_PROJ, OUT_GATE, OUT_FINAL, IN_PROJ, IN_GATE, IN_FINAL, WEIGHTS = 0, 512, 640, 768, 1280, 1408, 1536


def weights_kernel(*refs):
    start = 0
    for weight_ref in refs[:-1]:
        weight, width = weight_ref[...], weight_ref.shape[1]
        if start in (IN_PROJ, IN_GATE):
            weight = weight - jnp.mean(weight, axis=0, keepdims=True)
        refs[-1][:, pl.ds(start, width)] = halved(weight)
        start += width


def to_lines(target, base, tile, slot, slots, line):
    for k in range(SIDE):
        target[pl.ds(base + line * k + MAIN * slot, MAIN), :] = tile[MAIN * k : MAIN * (k + 1)]
    for e in range(REST):
        target[pl.ds(base + MAIN * slots + REST * slot + e, SIDE, stride=line), :] = tile[
            rest_rows(e) : rest_rows(e) + SIDE
        ]


RIGHT_LINE = 24
LENGTH = SIDE * WIDTH
GROUP = 4


def add_terms(tiles, other, proj_weight, before_ref, outer_ref, lines_ref, right_lines_ref, left_ref, right_ref):
    for slot in range(SPLIT):
        to_lines(lines_ref, 0, tiles[slot].astype(jnp.float32), slot, SPLIT, WIDTH)
    to_lines(right_lines_ref, 0, tiles[0].astype(jnp.float32), 0, 2, RIGHT_LINE)
    to_lines(right_lines_ref, 0, tiles[other].astype(jnp.float32), 1, 2, RIGHT_LINE)
    raw = jnp.concatenate([lines_ref[...], right_lines_ref[...]], axis=0)
    centred = split_lines(raw)[0]
    scale = scale_of(centred)
    proj = dot(centred[:LENGTH], proj_weight[:, :256]) * scale[:LENGTH]
    left_ref[...] = gated(proj[:, :128], proj[:, 128:])
    proj = dot(centred[LENGTH:], proj_weight[:, 256:]) * scale[LENGTH:]
    right_ref[...] = gated(proj[:, :128], proj[:, 128:])

    for g in range(2 * SIDE // GROUP):
        at = [pl.ds((g * GROUP + t) * WIDTH, WIDTH) for t in range(GROUP)]
        sums = [None if before_ref is None else before_ref[at[t], :] for t in range(GROUP)]
        for k in range(SIDE):
            rows = left_ref[pl.ds(k * WIDTH, WIDTH), :]
            for t in range(GROUP):
                one = right_ref[pl.ds(k * RIGHT_LINE + g * GROUP + t, 1), :]
                term = rows * jnp.broadcast_to(one, rows.shape)
                sums[t] = term if sums[t] is None else sums[t] + term
        for t in range(GROUP):
            outer_ref[at[t], :] = sums[t]


def split_lines(raw):
    valid = raw < 0.5 * MASKED
    return jnp.where(valid, raw, 0.0), valid


def other_slot():
    before = lax.rem(lax.axis_index("row") - lax.axis_index("col") + SPLIT, SPLIT)
    place = jnp.int32(0)
    for number, step in enumerate(STEPS):
        place = jnp.where(before == step, number + 1, place)
    return place


def other_part():
    return jnp.bitwise_xor(lax.axis_index("row"), lax.axis_index("col"))


def first_kernel(tiles, out_proj_ref, outer_ref, *scratch):
    add_terms(tiles, other_slot(), halved(out_proj_ref[...]), None, outer_ref, *scratch)


def next_kernel(tiles, weights_ref, before_ref, outer_ref, *scratch):
    add_terms(tiles, other_slot(), weights_ref[:, pl.ds(OUT_PROJ, 512)], before_ref, outer_ref, *scratch)


def gate_kernel(tiles, own_ref, weights_ref, centred_ref, half_gate_ref, valid_ref, lines_ref):
    for slot in range(SPLIT):
        to_lines(lines_ref, 0, tiles[slot].astype(jnp.float32), slot, SPLIT, WIDTH)
    centred, valid = split_lines(lines_ref[...])
    centred_ref[...] = centred
    valid_ref[...] = jnp.where(valid, 1.0, 0.0)
    own = own_ref[...]
    own = own - jnp.mean(own, axis=-1, keepdims=True)
    to_lines(centred_ref, 0, own, 0, SPLIT, WIDTH)
    centred = centred_ref[...]
    half_gate_ref[...] = dot(centred, weights_ref[:, pl.ds(OUT_GATE, 128)]) * scale_of(centred)


def last_kernel(
    part0, part1, part2, part3, before_ref, centred0_ref, half_gate0_ref, valid0_ref, own_ref,
    weights_ref,
    result_ref,
    lines_ref, right_lines_ref, left_ref, right_ref, outer_ref, block_ref, left2_ref, right2_ref, change_ref, normed_ref,
    pieces_ref, flat_ref, flat2_ref,
):
    for number, tiles in enumerate((part0, part1, part3, part2)):
        @pl.when(other_part() == number)
        def _():
            for slot in range(SPLIT):
                to_lines(block_ref, 0, tiles[slot].astype(jnp.float32), slot, SPLIT, WIDTH)

    add_terms(
        part3, other_slot(), weights_ref[:, pl.ds(OUT_PROJ, 512)], before_ref, outer_ref,
        lines_ref, right_lines_ref, left_ref, right_ref,
    )

    def sums_of(slot):
        return [
            outer_ref[pl.ds(slot * MAIN * WIDTH, MAIN * WIDTH), :],
            outer_ref[pl.ds((2 * MAIN + REST * slot) * WIDTH, REST * WIDTH), :],
        ]

    centred1, valid1 = split_lines(block_ref[...])
    half_gate1 = dot(centred1, weights_ref[:, pl.ds(OUT_GATE, 128)]) * scale_of(centred1)
    half_gate = jnp.concatenate([half_gate0_ref[...], half_gate1], axis=0)
    centred = jnp.concatenate([centred0_ref[...], centred1], axis=0)
    sums = centre(jnp.concatenate(sums_of(1) + sums_of(0), axis=0))
    change = gated(half_gate, dot(sums, weights_ref[:, pl.ds(OUT_FINAL, 128)]) * scale_of(sums))
    mid = centred + change
    scale = scale_of_whole(mid)
    change_ref[...] = change[:LENGTH]
    normed_ref[...] = mid[:LENGTH] * scale[:LENGTH]
    proj = dot(mid[:LENGTH], weights_ref[:, pl.ds(IN_PROJ + 256, 256)]) * scale[:LENGTH]
    right2_ref[...] = valid0_ref[...] * gated(proj[:, :128], proj[:, 128:])
    proj = dot(mid[LENGTH:], weights_ref[:, pl.ds(IN_PROJ, 256)]) * scale[LENGTH:]
    left2_ref[...] = jnp.where(valid1, gated(proj[:, :128], proj[:, 128:]), 0.0)

    for j in range(SIDE):
        right = right2_ref[pl.ds(j * WIDTH, WIDTH), :]
        for i in range(SIDE):
            product = left2_ref[pl.ds(i * WIDTH, WIDTH), :] * right
            folded = product[:8]
            for t in range(1, WIDTH // 8):
                folded = folded + product[8 * t : 8 * (t + 1)]
            at = MAIN * j + i if i < MAIN else rest_rows(i - MAIN) + j
            pieces_ref[pl.ds(8 * at, 8), :] = folded
    inner = pieces_ref[pl.ds(0, ROWS, stride=8), :]
    for t in range(1, 8):
        inner = inner + pieces_ref[pl.ds(t, ROWS, stride=8), :]

    def own_rows(source_ref, flat_ref):
        for k in range(SIDE):
            flat_ref[pl.ds(MAIN * k, MAIN), :] = source_ref[pl.ds(WIDTH * k, MAIN), :]
        for e in range(REST):
            flat_ref[pl.ds(rest_rows(e), SIDE), :] = source_ref[pl.ds(MAIN * SPLIT + e, SIDE, stride=WIDTH), :]
        return flat_ref[...]

    mid = own_ref[...] + own_rows(change_ref, flat_ref)
    half_gate = dot(own_rows(normed_ref, flat2_ref), weights_ref[:, pl.ds(IN_GATE, 128)])
    inner = centre(inner)
    result = mid + gated(half_gate, dot(inner, weights_ref[:, pl.ds(IN_FINAL, 128)]) * scale_of(inner))
    for k in range(SIDE):
        result_ref[pl.ds(0, MAIN), k, :] = result[MAIN * k : MAIN * (k + 1)]
        for e in range(REST):
            result_ref[MAIN + e, pl.ds(k, 1), :] = result[rest_rows(e) + k : rest_rows(e) + k + 1]


def swapped(value, rows, cols):
    pairs = [
        (r * SPLIT + c, (r ^ rows) * SPLIT + (c ^ cols)) for r in range(SPLIT) for c in range(SPLIT)
    ]
    return lax.ppermute(value, ("row", "col"), pairs)


STEPS = (1, 2, 3)


def shifted(value, step, cols=0):
    pairs = [
        (r * SPLIT + c, (r + step) % SPLIT * SPLIT + (c ^ cols)) for r in range(SPLIT) for c in range(SPLIT)
    ]
    return lax.ppermute(value, ("row", "col"), pairs)


def in_vmem(value):
    return pltpu.with_memory_space_constraint(value, pltpu.VMEM)


def call(kernel, name, cycles, out, scratch, *operands, grant=32 << 20, **more):
    return pl.pallas_call(
        kernel,
        out_shape=out,
        scratch_shapes=[pltpu.VMEM(one, jnp.float32) if isinstance(one, tuple) else one for one in scratch],
        cost_estimate=pl.CostEstimate(flops=cycles, bytes_accessed=0, transcendentals=0),
        compiler_params=pltpu.CompilerParams(vmem_limit_bytes=grant),
        name=name,
        **more,
    )(*operands)


def compact_plan(pair, pair_mask, *weights):
    f32 = jnp.float32
    tile, own = call(
        pack_kernel, "pack", 1000, (pltpu.VMEM((ROWS, 128), jnp.bfloat16), pltpu.VMEM((ROWS, 128), f32)),
        [(ROWS, 128), pair.shape, pltpu.VMEM(pair_mask.shape, jnp.int32), pltpu.SemaphoreType.DMA((2,))],
        pair, pair_mask, grant=None, in_specs=2 * [pl.BlockSpec(memory_space=pl.ANY)],
    )
    around = [tile] + [shifted(tile, step) for step in STEPS]
    aslant = shifted(tile, STEPS[2], 3)
    early = jnp.stack(around[:3])
    swapped_early = swapped(early, 0, 3)
    late, _ = lax.optimization_barrier((around[3], early))
    part0 = jnp.concatenate([early, late[None]])
    lines = pltpu.VMEM((LENGTH, 128), f32)
    sums = pltpu.VMEM((2 * LENGTH, 128), f32)
    work = [(LENGTH, 128), (SIDE * RIGHT_LINE, 128), (LENGTH, 128), (SIDE * RIGHT_LINE, 128)]
    cost = 1 << 10
    outer = call(first_kernel, "first", cost, sums, work, in_vmem(part0), in_vmem(weights[0]))
    outer, *weights = lax.optimization_barrier((outer, *weights))
    weights = call(
        weights_kernel, "weights", 1000, pltpu.VMEM((2 * 128, WEIGHTS), jnp.bfloat16), [], *weights, grant=None
    )
    weights = in_vmem(weights)
    centred0, gate0, valid0 = call(
        gate_kernel, "gate", cost, (lines, lines, lines), [(LENGTH, 128)], in_vmem(part0), in_vmem(own), weights
    )
    aslant, swapped_early, outer, gate0 = lax.optimization_barrier((aslant, swapped_early, outer, gate0))
    part2 = jnp.concatenate([swapped_early, aslant[None]])
    part1 = swapped(part0, 0, 1)
    outer = call(next_kernel, "second", cost, sums, work, in_vmem(part1), weights, in_vmem(outer))
    part3 = swapped(part2, 0, 1)
    outer = call(next_kernel, "third", cost, sums, work, in_vmem(part2), weights, in_vmem(outer))
    part3, outer = lax.optimization_barrier((part3, outer))
    return call(
        last_kernel, "last", cost, jax.ShapeDtypeStruct(pair.shape, f32),
        work + [(2 * LENGTH, 128)] + 5 * [(LENGTH, 128)] + [(8 * ROWS, 128), (ROWS, 128), (ROWS, 128)],
        *map(in_vmem, (part0, part1, part2, part3, outer, centred0, gate0, valid0, own)),
        weights,
    )


def solution(mesh):
    def body(pair, *rest):
        compact = (
            mesh.shape["row"] == mesh.shape["col"] == SPLIT
            and pair.shape == (SIDE, SIDE, 128)
            and rest[1].shape == (128, 512)
        )
        return (compact_plan if compact else split_plan)(pair, *rest)

    return jax.shard_map(
        body,
        mesh=mesh,
        in_specs=(
            P(("grp", "row"), "col", None),
            P(("grp", "row"), "col"),
            P(),
            P(),
            P(),
            P(),
            P(),
            P(),
        ),
        out_specs=P(("grp", "row"), "col", None),
        check_vma=False,
    )
```
